32 devices in a mesh: sens: 4 (over y, x), par: 8 (over z, core).
Axes of the slice: x: 2, y: 2, z: 4, core: 2. Of those that a mesh axis runs over, the one named last changes fastest.
Arguments:
- records: float32 [16, 600, 224], P(None, 'sens'), may hold values from -6 to 6
- spec_real: float32 [225, 600, 1024], P(None, 'sens', 'par'), may hold values from -0.125 to 0.125
- spec_imag: float32 [225, 600, 1024], P(None, 'sens', 'par'), may hold values from -0.125 to 0.125
- prior_cov: float32 [224, 224], replicated, as said below
- sensor_map: int32 [600], replicated, may hold values from 0 to 599, each once
- inverse_rows: float32 [384, 224, 600], P('sens', 'par'), may hold values from -0.015625 to 0.015625
Outputs:
- update: float32 [16, 384], P('par', 'sens')
The draws below stay inside these ranges and needn't reach their ends.
Inputs may be any that keep to these rules, and one draw needn't show every extreme that they name: prior_cov is symmetric. sensor_map names every sensor once.
All inputs are finite; a program needn't handle non-finite values.
Results may differ from the reference program's by a relative error of at most 0.00013.
Values sent between devices are 32-bit elements; how exact they have to be, the bound alone decides.
No kernel may reach another device: no remote copies, remote signals or barrier semaphores. Data moves between devices by JAX's collectives and lax.ppermute only.
A program may use at most 128 MiB of HBM per device.

```python
import math
import jax
import jax.numpy as jnp
from jax import lax

SENS = 600
NT = 224
COLS = 16
NF = 225
PAR = 1024
ROWS = 384


def draw_prior_cov(key, part):
    sample = jax.random.normal(key, (NT, NT), jnp.float32)
    symmetric = (sample + sample.T) * (0.5 / math.sqrt(NT))
    return symmetric + 2.0 * jnp.eye(NT, dtype=jnp.float32)


def levels(key, extent, cuts, smallest, high):
    loudness, own = 1.0, jax.random.fold_in(key, 6)
    for position, shards_of in cuts:
        heights = jnp.exp(jax.random.uniform(jax.random.fold_in(own, position), (shards_of,), jnp.float32, smallest / len(cuts), high / len(cuts)))
        loudness = loudness * jnp.repeat(heights, extent[position] // shards_of).reshape([-1 if axis == position else 1 for axis in range(len(extent))])
    return loudness


def bell_draw(rng, shape, scale, most, shards=(), kind=jnp.bfloat16):
    drawn = scale * jax.random.normal(rng, shape, jnp.float32)
    if shards:
        drawn = drawn * levels(rng, shape, shards, -0.22, 0.18)
    return jnp.clip(drawn, -most, most).astype(kind)


def setup_inputs(seed: int = 0) -> dict:
    streams_of = jax.random.split(jax.random.key(seed), 7)
    records = bell_draw(streams_of[0], (COLS, SENS, NT), 1.0, 6.0, ((1, 4),), jnp.float32)
    spec_real = bell_draw(streams_of[1], (NF, SENS, PAR), (2 * SENS + PAR) ** -0.5, 0.125, ((1, 4), (2, 8)), jnp.float32)
    spec_imag = bell_draw(streams_of[2], (NF, SENS, PAR), (2 * SENS + PAR) ** -0.5, 0.125, ((1, 4), (2, 8)), jnp.float32)
    prior_cov = draw_prior_cov(jax.random.fold_in(streams_of[6], 71), 0)
    sensor_map = jax.random.permutation(streams_of[4], SENS).astype(jnp.int32)
    inverse_rows = bell_draw(streams_of[5], (ROWS, NT, SENS), (NT * SENS) ** -0.5, 0.015625, ((0, 4), (1, 8)), jnp.float32)
    return dict(records=records, spec_real=spec_real, spec_imag=spec_imag, prior_cov=prior_cov, sensor_map=sensor_map, inverse_rows=inverse_rows)


highest = lax.Precision.HIGHEST


def reference(records, spec_real, spec_imag, prior_cov, sensor_map, inverse_rows):
    length = 2 * NT
    rec_spec = jnp.fft.rfft(records, n=length, axis=2)
    rec_real = jnp.real(rec_spec)
    rec_imag = jnp.imag(rec_spec)
    adj_real = jnp.einsum('csw,wsp->cpw', rec_real, spec_real, precision=highest) + jnp.einsum('csw,wsp->cpw', rec_imag, spec_imag, precision=highest)
    adj_imag = jnp.einsum('csw,wsp->cpw', rec_imag, spec_real, precision=highest) - jnp.einsum('csw,wsp->cpw', rec_real, spec_imag, precision=highest)
    adjoint = jnp.fft.irfft(lax.complex(adj_real, adj_imag), n=length, axis=2)[:, :, :NT]
    prior_field = jnp.dot(adjoint, prior_cov, precision=highest, preferred_element_type=jnp.float32)
    field_spec = jnp.fft.rfft(prior_field, n=length, axis=2)
    field_real = jnp.real(field_spec)
    field_imag = jnp.imag(field_spec)
    pred_real = jnp.einsum('cpw,wsp->csw', field_real, spec_real, precision=highest) - jnp.einsum('cpw,wsp->csw', field_imag, spec_imag, precision=highest)
    pred_imag = jnp.einsum('cpw,wsp->csw', field_imag, spec_real, precision=highest) + jnp.einsum('cpw,wsp->csw', field_real, spec_imag, precision=highest)
    predicted = jnp.fft.irfft(lax.complex(pred_real, pred_imag), n=length, axis=2)[:, :, :NT]
    permuted = jnp.take(predicted, sensor_map, axis=1)
    return jnp.einsum('rtk,ckt->cr', inverse_rows, permuted, precision=highest)
```

```python
import functools

import jax
import jax.numpy as jnp
import numpy as np
from jax import lax
from jax.experimental import pallas as pl
from jax.experimental.pallas import tpu as pltpu
from jax.sharding import PartitionSpec as P

F32 = jnp.float32
BF16 = jnp.bfloat16
LANES = 128


def round_up(value, step):
    return (value + step - 1) // step * step


def split(value):
    high = value.astype(BF16)
    low = (value - high.astype(F32)).astype(BF16)
    return high, low


def dot(left, right):
    return lax.dot_general(left, right, (((1,), (0,)), ((), ())), preferred_element_type=F32)


def dot_nt(left, right):
    return lax.dot_general(left, right, (((1,), (1,)), ((), ())), preferred_element_type=F32)


def split_host(table):
    high = table.astype(np.float32).astype(jnp.bfloat16)
    low = (table - high.astype(np.float64)).astype(jnp.bfloat16)
    return high, low


def forward_table(steps, bins, padded):
    length = 2 * steps
    phase = 2.0 * np.pi * ((np.arange(bins)[:, None] * np.arange(steps)[None, :]) % length) / length
    table = np.zeros((2 * padded, steps))
    table[:bins] = np.cos(phase)
    table[padded : padded + bins] = -np.sin(phase)
    return table


def inverse_table(steps, bins, padded):
    length = 2 * steps
    phase = 2.0 * np.pi * ((np.arange(steps)[:, None] * np.arange(bins)[None, :]) % length) / length
    weight = np.full((bins,), 2.0)
    weight[0] = 1.0
    weight[-1] = 1.0
    weight = weight / length
    table = np.zeros((steps, 2 * padded))
    table[:, :bins] = np.cos(phase) * weight
    table[:, padded : padded + bins] = -np.sin(phase) * weight
    return table


def block_of(bins, most):
    return max(size for size in range(1, most + 1) if bins % size == 0)


class Packing:
    def __init__(self, cols, sens_dev):
        self.cols = cols
        self.sens_dev = sens_dev
        self.full = sens_dev // LANES
        self.rest = sens_dev % LANES
        self.share = LANES // self.rest if self.rest else 1
        self.rest_rows = -(-cols // self.share) if self.rest else 0
        self.rows = self.full * cols + self.rest_rows
        self.width = LANES * (self.full + (1 if self.rest else 0))


def adjoint_kernel(mask_ref, rec_ref, fh_ref, fl_ref, ih_ref, il_ref, sr_ref, si_ref, *rest):
    outs, (rec_spec, adj) = rest[:-2], rest[-2:]
    step = pl.program_id(0)
    cols = rec_ref.shape[0]
    block, sens_dev, par_dev = sr_ref.shape
    bins = rec_spec.shape[0]
    padded = adj.shape[1] // 2
    half = cols // 2

    @pl.when(step == 0)
    def _():
        fh, fl = fh_ref[...], fl_ref[...]
        for k in range(cols):
            rh, rl = split(rec_ref[jnp.bitwise_xor(k, mask_ref[k // half])])
            value = dot_nt(fh, rh) + (dot_nt(fl, rh) + dot_nt(fh, rl))
            rec_spec[:, k, :] = value[:bins]
            rec_spec[:, cols + k, :] = value[padded : padded + bins]
        zeros = jnp.zeros((cols, padded - bins, par_dev), F32)
        adj[:, bins:padded, :] = zeros
        adj[:, padded + bins :, :] = zeros

    for i in range(block):
        w = step * block + i
        xh, xl = split(rec_spec[w])
        sh, sl = split(jnp.concatenate([sr_ref[i], si_ref[i]], axis=1))
        both = dot(jnp.concatenate([xh, xl], axis=0), sh)
        value = both[: 2 * cols] + both[2 * cols :] + dot(xh, sl)
        adj[:, pl.ds(w, 1), :] = (value[:cols, :par_dev] + value[cols:, par_dev:])[:, None, :]
        adj[:, pl.ds(padded + w, 1), :] = (value[cols:, :par_dev] - value[:cols, par_dev:])[:, None, :]

    @pl.when(step == pl.num_programs(0) - 1)
    def _():
        ih, il = ih_ref[...], il_ref[...]
        per = cols // len(outs)
        for k in range(0, cols, 2):
            ah, al = split(jnp.concatenate([adj[k], adj[k + 1]], axis=1))
            value = dot(ih, ah) + (dot(il, ah) + dot(ih, al))
            outs[k // per][k % per] = value[:, :par_dev]
            outs[(k + 1) // per][(k + 1) % per] = value[:, par_dev:]


def forward_kernel(packing, mask_ref, th_ref, tl_ref, ih_ref, il_ref, *rest):
    (keep_ref, send_ref, field, pred, left) = rest[-5:]
    sr_ref, si_ref = rest[-7:-5]
    pieces = rest[:-7]
    step = pl.program_id(0)
    cols = packing.cols
    block, sens_dev, par_dev = sr_ref.shape
    bins = field.shape[0]
    padded = pred.shape[1] // 2
    half = cols // 2
    full, width = packing.full, packing.full * LANES

    @pl.when(step == 0)
    def _():
        th, tl = th_ref[...], tl_ref[...]
        per = cols // len(pieces)
        for k in range(0, cols, 2):
            first, second = pieces[k // per][k % per], pieces[(k + 1) // per][(k + 1) % per]
            ah, al = split(jnp.concatenate([first, second], axis=1))
            value = dot(th, ah) + (dot(tl, ah) + dot(th, al))
            for j in range(2):
                c = jnp.bitwise_xor(k + j, mask_ref[k // half])
                part = value[:, j * par_dev : (j + 1) * par_dev]
                field[:, pl.ds(c, 1), :] = part[:bins][:, None, :]
                field[:, pl.ds(cols + c, 1), :] = part[padded : padded + bins][:, None, :]
        zeros = jnp.zeros((cols, padded - bins, sens_dev), F32)
        pred[:, bins:padded, :] = zeros
        pred[:, padded + bins :, :] = zeros

    for i in range(block):
        w = step * block + i
        x = field[w]
        turned = jnp.concatenate([-x[cols:], x[:cols]], axis=0)
        xh, xl = split(jnp.concatenate([x, turned], axis=1))
        sh, sl = split(jnp.concatenate([sr_ref[i], si_ref[i]], axis=1))
        both = dot_nt(jnp.concatenate([xh, xl], axis=0), sh)
        value = both[: 2 * cols] + both[2 * cols :] + dot_nt(xh, sl)
        pred[:, pl.ds(w, 1), :] = value[:cols][:, None, :]
        pred[:, pl.ds(padded + w, 1), :] = value[cols:][:, None, :]

    @pl.when(step == pl.num_programs(0) - 1)
    def _():
        ih, il = ih_ref[...], il_ref[...]
        rows = packing.rows
        count = ih.shape[0] // 2
        for c in range(cols):
            ph, pl_low = split(pred[c])
            value = dot(ih, ph) + (dot(il, ph) + dot(ih, pl_low))
            for f in range(full):
                part = value[:, f * LANES : (f + 1) * LANES]
                keep_ref[pl.ds(c * full + f, count, stride=rows), :] = part[:count]
                send_ref[pl.ds(c * full + f, count, stride=rows), :] = part[count:]
            if packing.rest:
                place = c % packing.share
                pieces_of = [value[:, width:]]
                if place:
                    pieces_of = [jnp.zeros((2 * count, place * packing.rest), F32)] + pieces_of
                after = LANES - (place + 1) * packing.rest
                if after:
                    pieces_of = pieces_of + [jnp.zeros((2 * count, after), F32)]
                part = jnp.concatenate(pieces_of, axis=1)
                if place == 0:
                    left[...] = part
                else:
                    left[...] += part
                if place == packing.share - 1 or c == cols - 1:
                    row = cols * full + c // packing.share
                    keep_ref[pl.ds(row, count, stride=rows), :] = left[:count]
                    send_ref[pl.ds(row, count, stride=rows), :] = left[count:]


def prepare_kernel(packing, index_ref, map_ref, prior_ref, fh_ref, fl_ref, inv_ref, rows_ref,
                   oh_ref, ol_ref, th_ref, tl_ref, ih_ref, il_ref, select, table):
    step = pl.program_id(0)
    blocks = oh_ref.shape[2] // packing.width
    times = rows_ref.shape[1]
    count = rows_ref.shape[0]

    @pl.when(step == 0)
    def _():
        lane = lax.broadcasted_iota(jnp.int32, (1, packing.width), 1)
        width = packing.full * LANES
        if packing.rest:
            beyond = lane - width
            folded = width + lax.rem(jnp.maximum(beyond, 0), packing.rest)
            local = jnp.where(beyond >= 0, folded, lane)
            valid = beyond < packing.share * packing.rest
        else:
            local = lane
            valid = lane >= 0
        for m in range(blocks):
            owner = jnp.bitwise_xor(index_ref[0], m)
            wanted = jnp.where(valid, owner * packing.sens_dev + local, -1)
            hit = map_ref[...] == wanted
            select[:, m * packing.width : (m + 1) * packing.width] = jnp.where(hit, 1.0, 0.0).astype(BF16)
        ph, pl_low = split(prior_ref[...])
        folded_table = dot_nt(fh_ref[...], ph) + (dot_nt(fl_ref[...], ph) + dot_nt(fh_ref[...], pl_low))
        th, tl = split(folded_table)
        th_ref[...] = th
        tl_ref[...] = tl
        par = inv_ref.shape[0]
        pairs = par // 2
        for r in range(2):
            for d in range(pairs):
                z = lax.rem(index_ref[1] // 2 + d, pairs)
                core = jnp.bitwise_xor(lax.rem(index_ref[1], 2), r)
                j = r * pairs + d
                table[j * times : (j + 1) * times, :] = inv_ref[2 * z + core]
        ih, il = split(table[...])
        ih_ref[...] = ih
        il_ref[...] = il

    group = block_of(times, 7)
    for t in range(0, times, group):
        parts = []
        for g in range(group):
            parts.extend(split(rows_ref[:, t + g, :]))
        moved = dot(jnp.concatenate(parts, axis=0), select[...]).astype(BF16)
        for g in range(group):
            oh_ref[t + g] = moved[2 * g * count : (2 * g + 1) * count]
            ol_ref[t + g] = moved[(2 * g + 1) * count : (2 * g + 2) * count]


def update_kernel(packing, oh_ref, ol_ref, *rest):
    gathered, out_ref = rest[:-1], rest[-1]
    times = oh_ref.shape[0]
    cols, rows, full = packing.cols, packing.rows, packing.full
    total = jnp.zeros(out_ref.shape, F32)
    if packing.rest:
        row = lax.broadcasted_iota(jnp.int32, (cols, LANES), 0)
        lane = lax.broadcasted_iota(jnp.int32, (cols, LANES), 1)
        own = lax.rem(row, packing.share) == lane // packing.rest
        shared = row // packing.share
    for t in range(times):
        for m, ref in enumerate(gathered):
            held = ref[t * rows : (t + 1) * rows, :]
            parts = []
            if full == 1:
                parts.append(held[:cols])
            elif full > 1:
                wide = held[: cols * full].reshape(cols, full, LANES)
                parts.extend(wide[:, f, :] for f in range(full))
            if packing.rest:
                spread = jnp.zeros((cols, LANES), F32)
                for j in range(packing.rest_rows):
                    line = held[cols * full + j : cols * full + j + 1]
                    spread = jnp.where(own & (shared == j), line, spread)
                parts.append(spread)
            xh, xl = split(jnp.concatenate(parts, axis=1))
            place = slice(m * packing.width, (m + 1) * packing.width)
            both = dot_nt(jnp.concatenate([xh, xl], axis=0), oh_ref[t, :, place])
            total = total + (both[:cols] + both[cols:] + dot_nt(xh, ol_ref[t, :, place]))
    out_ref[...] = total


def whole(array):
    return pl.BlockSpec(array.shape, lambda *_: (0,) * array.ndim)


def swap(size, mask):
    return [(k, k ^ mask) for k in range(size)]


def reduce_quarters(keep, send, first, second, size):
    per = keep.shape[0] // 2
    near = keep + lax.ppermute(send, "sens", swap(size, first))
    here = near[:per] + lax.ppermute(near[per:], "sens", swap(size, second))
    over = lax.ppermute(here, "sens", swap(size, second))
    back = lax.ppermute(here, "sens", swap(size, first))
    return [here, over, back, lax.ppermute(over, "sens", swap(size, first))]


def shards(records, spec_real, spec_imag, prior_cov, sensor_map, inverse_rows):
    cols, sens_dev, steps = records.shape
    bins, _, par_dev = spec_real.shape
    padded = round_up(bins, 8)
    sens, par = lax.axis_size("sens"), lax.axis_size("par")
    sens_index, par_index = lax.axis_index("sens"), lax.axis_index("par")
    packing = Packing(cols, sens_dev)
    rows_dev, times, sensors = inverse_rows.shape
    quarters = sens == 4 and cols % 8 == 0
    limit = 56 * 2**20

    fwd = forward_table(steps, bins, padded)
    inv = inverse_table(steps, bins, padded)
    fh, fl = (jnp.asarray(part) for part in split_host(fwd))
    ih, il = (jnp.asarray(part) for part in split_host(inv))
    inv_blocks = jnp.asarray(inv.reshape(par, times, 2 * padded).astype(np.float32))

    if quarters:
        bit0, bit1 = sens_index & 1, sens_index >> 1
        unit = cols // 8
        mask = jnp.stack([(2 * bit0 + bit1) * unit, (2 * bit1 + bit0) * unit]).astype(jnp.int32)
        n_out = 4
    else:
        mask = jnp.zeros((2,), jnp.int32)
        n_out = 1

    block = block_of(bins, 15)
    grid = (bins // block,)
    spec_block = pl.BlockSpec((block, sens_dev, par_dev), lambda i: (i, 0, 0))
    smem = pl.BlockSpec(memory_space=pltpu.SMEM)
    phase_cost = pl.CostEstimate(
        flops=24 * cols * bins * sens_dev * par_dev, bytes_accessed=8 * bins * sens_dev * par_dev, transcendentals=0
    )
    out_a = [jax.ShapeDtypeStruct((cols // n_out, steps, par_dev), F32)] * n_out
    parts = pl.pallas_call(
        adjoint_kernel,
        grid=grid,
        in_specs=[smem, whole(records), whole(fh), whole(fl), whole(ih), whole(il), spec_block, spec_block],
        out_specs=[whole(shape) for shape in out_a],
        out_shape=out_a,
        scratch_shapes=[
            pltpu.VMEM((bins, 2 * cols, sens_dev), F32),
            pltpu.VMEM((cols, 2 * padded, par_dev), F32),
        ],
        compiler_params=pltpu.CompilerParams(vmem_limit_bytes=limit),
        cost_estimate=phase_cost,
        name="adjoint",
    )(mask, records, fh, fl, ih, il, spec_real, spec_imag)

    index = jnp.stack([sens_index, par_index]).astype(jnp.int32)
    row_block = block_of(rows_dev, 32)
    width = sens * packing.width
    moved = jax.ShapeDtypeStruct((times, rows_dev, width), BF16)
    folded = jax.ShapeDtypeStruct((2 * padded, steps), BF16)
    turned = jax.ShapeDtypeStruct((steps, 2 * padded), BF16)
    map_column = sensor_map.reshape(sensors, 1)
    oh, ol, th, tl, ih2, il2 = pl.pallas_call(
        functools.partial(prepare_kernel, packing),
        grid=(rows_dev // row_block,),
        in_specs=[
            smem,
            whole(map_column),
            whole(prior_cov),
            whole(fh),
            whole(fl),
            whole(inv_blocks),
            pl.BlockSpec((row_block, times, sensors), lambda i: (i, 0, 0)),
        ],
        out_specs=[pl.BlockSpec((times, row_block, width), lambda i: (0, i, 0))] * 2
        + [whole(folded)] * 2
        + [whole(turned)] * 2,
        out_shape=[moved, moved, folded, folded, turned, turned],
        scratch_shapes=[pltpu.VMEM((sensors, width), BF16), pltpu.VMEM((steps, 2 * padded), F32)],
        compiler_params=pltpu.CompilerParams(vmem_limit_bytes=limit),
        cost_estimate=pl.CostEstimate(
            flops=4 * rows_dev * times * sensors * width, bytes_accessed=8 * rows_dev * times * sensors, transcendentals=0
        ),
        name="prepare",
    )(index, map_column, prior_cov, fh, fl, inv_blocks, inverse_rows)

    if quarters:
        pieces = reduce_quarters(parts[0], parts[1], 1, 2, sens) + reduce_quarters(parts[2], parts[3], 2, 1, sens)
    else:
        pieces = [lax.psum(parts[0], "sens")]

    shard_rows = times * packing.rows
    half = jax.ShapeDtypeStruct((par // 2 * shard_rows, LANES), F32)
    keep, send = pl.pallas_call(
        functools.partial(forward_kernel, packing),
        grid=grid,
        in_specs=[smem, whole(th), whole(tl), whole(ih2), whole(il2)]
        + [whole(piece) for piece in pieces]
        + [spec_block, spec_block],
        out_specs=[whole(half)] * 2,
        out_shape=[half, half],
        scratch_shapes=[
            pltpu.VMEM((bins, 2 * cols, par_dev), F32),
            pltpu.VMEM((cols, 2 * padded, sens_dev), F32),
            pltpu.VMEM((steps, LANES), F32),
        ],
        compiler_params=pltpu.CompilerParams(vmem_limit_bytes=limit),
        cost_estimate=phase_cost,
        name="forward",
    )(mask, th, tl, ih2, il2, *pieces, spec_real, spec_imag)

    pair = keep + lax.ppermute(send, "par", swap(par, 1))
    mine = pair[:shard_rows]
    for d in range(1, par // 2):
        there = pair[d * shard_rows : (d + 1) * shard_rows]
        mine = mine + lax.ppermute(there, "par", [(k, (k + 2 * d) % par) for k in range(par)])
    gathered = [mine] + [lax.ppermute(mine, "sens", swap(sens, m)) for m in range(1, sens)]

    result = jax.ShapeDtypeStruct((cols, rows_dev), F32)
    partial = pl.pallas_call(
        functools.partial(update_kernel, packing),
        out_shape=result,
        compiler_params=pltpu.CompilerParams(vmem_limit_bytes=limit),
        cost_estimate=pl.CostEstimate(
            flops=6 * rows_dev * times * cols * width, bytes_accessed=4 * rows_dev * times * width, transcendentals=0
        ),
        name="update",
    )(oh, ol, *gathered)
    per_dev = cols // par
    spread = lax.all_to_all(partial.reshape(par, per_dev, rows_dev), "par", 0, 0)
    return jnp.sum(spread, axis=0)


def solution(mesh):
    return jax.shard_map(
        shards,
        mesh=mesh,
        in_specs=(
            P(None, "sens", None),
            P(None, "sens", "par"),
            P(None, "sens", "par"),
            P(),
            P(),
            P("sens", "par", None),
        ),
        out_specs=P("par", "sens"),
        check_vma=False,
    )
```

```python
import functools

import jax
import jax.numpy as jnp
import numpy as np
from jax import lax
from jax.experimental import pallas as pl
from jax.experimental.pallas import tpu as pltpu
from jax.sharding import PartitionSpec as P

F32 = jnp.float32
BF16 = jnp.bfloat16
LANES = 128


def round_up(value, step):
    return (value + step - 1) // step * step


def split(value):
    high = value.astype(BF16)
    low = (value - high.astype(F32)).astype(BF16)
    return high, low


def dot(left, right):
    return lax.dot_general(left, right, (((1,), (0,)), ((), ())), preferred_element_type=F32)


def dot_nt(left, right):
    return lax.dot_general(left, right, (((1,), (1,)), ((), ())), preferred_element_type=F32)


def split_host(table):
    high = table.astype(np.float32).astype(jnp.bfloat16)
    low = (table - high.astype(np.float64)).astype(jnp.bfloat16)
    return high, low


def forward_table(steps, bins, padded):
    length = 2 * steps
    phase = 2.0 * np.pi * ((np.arange(bins)[:, None] * np.arange(steps)[None, :]) % length) / length
    table = np.zeros((2 * padded, steps))
    table[:bins] = np.cos(phase)
    table[padded : padded + bins] = -np.sin(phase)
    return table


def inverse_table(steps, bins, padded):
    length = 2 * steps
    phase = 2.0 * np.pi * ((np.arange(steps)[:, None] * np.arange(bins)[None, :]) % length) / length
    weight = np.full((bins,), 2.0)
    weight[0] = 1.0
    weight[-1] = 1.0
    weight = weight / length
    table = np.zeros((steps, 2 * padded))
    table[:, :bins] = np.cos(phase) * weight
    table[:, padded : padded + bins] = -np.sin(phase) * weight
    return table


def block_of(bins, most):
    return max(size for size in range(1, most + 1) if bins % size == 0)


class Packing:
    def __init__(self, cols, sens_dev):
        self.cols = cols
        self.sens_dev = sens_dev
        self.full = sens_dev // LANES
        self.rest = sens_dev % LANES
        self.share = LANES // self.rest if self.rest else 1
        self.rest_rows = -(-cols // self.share) if self.rest else 0
        self.rows = self.full * cols + self.rest_rows
        self.width = LANES * (self.full + (1 if self.rest else 0))


def lane_tiles(value):
    rows, columns = value.shape
    tiles = []
    for start in range(0, columns, LANES):
        tile = value[:, start : start + LANES]
        short = LANES - tile.shape[1]
        if short:
            tile = jnp.concatenate([tile, jnp.zeros((rows, short), value.dtype)], axis=1)
        tiles.append(tile)
    return tiles


def spec_copies(hbm_refs, vmem_refs, sems, chunk, block):
    part = pl.ds(chunk * block, block)
    return [
        pltpu.make_async_copy(hbm.at[part], vmem.at[part], sems.at[j, chunk])
        for j, (hbm, vmem) in enumerate(zip(hbm_refs, vmem_refs))
    ]


def start_all(hbm_refs, vmem_refs, sems, chunks, block):
    for chunk in range(chunks):
        for copy in spec_copies(hbm_refs, vmem_refs, sems, chunk, block):
            copy.start()


def adjoint_kernel(mask_ref, rec_ref, fh_ref, fl_ref, ih_ref, il_ref, sr_hbm, si_hbm, *rest):
    outs, (sr_ref, si_ref, sems, spread, rec_spec, adj) = rest[:-6], rest[-6:]
    sens_dev, cols, steps = rec_ref.shape
    bins, _, par_dev = sr_ref.shape
    chunks = sems.shape[1]
    block = bins // chunks
    padded = adj.shape[0] // cols // 2
    tall = 2 * padded
    half = cols // 2
    start_all((sr_hbm, si_hbm), (sr_ref, si_ref), sems, chunks, block)

    every = rec_ref[...].reshape(sens_dev * cols, steps)
    for f, tile in enumerate(lane_tiles(every)):
        spread[f] = tile
    for row in list(range(bins, padded)) + list(range(padded + bins, tall)):
        adj[pl.ds(row, cols, stride=tall), :] = jnp.zeros((cols, par_dev), F32)

    def column(c, _):
        own = [spread[f, pl.ds(c, sens_dev, stride=cols), :] for f in range(spread.shape[0])]
        rh, rl = split(jnp.concatenate(own, axis=1)[:, :steps])
        fh, fl = fh_ref[...], fl_ref[...]
        value = dot_nt(fh, rh) + (dot_nt(fl, rh) + dot_nt(fh, rl))
        for f, tile in enumerate(lane_tiles(value)):
            rec_spec[f, pl.ds(c, bins, stride=2 * cols), :] = tile[:bins]
            rec_spec[f, pl.ds(cols + c, bins, stride=2 * cols), :] = tile[padded : padded + bins]
        return 0

    lax.fori_loop(0, cols, column, 0)

    def chunk_body(chunk, _):
        for copy in spec_copies((sr_hbm, si_hbm), (sr_ref, si_ref), sems, chunk, block):
            copy.wait()
        for i in range(block):
            w = chunk * block + i
            at = pl.ds(pl.multiple_of(w * 2 * cols, 8), 2 * cols)
            x = jnp.concatenate([rec_spec[f, at, :] for f in range(rec_spec.shape[0])], axis=1)[:, :sens_dev]
            xh, xl = split(x)
            sh, sl = split(jnp.concatenate([sr_ref[w], si_ref[w]], axis=1))
            both = dot(jnp.concatenate([xh, xl], axis=0), sh)
            value = both[: 2 * cols] + both[2 * cols :] + dot(xh, sl)
            adj[pl.ds(w, cols, stride=tall), :] = value[:cols, :par_dev] + value[cols:, par_dev:]
            adj[pl.ds(padded + w, cols, stride=tall), :] = value[cols:, :par_dev] - value[:cols, par_dev:]
        return 0

    lax.fori_loop(0, chunks, chunk_body, 0)

    per = cols // len(outs)
    for o, out in enumerate(outs):
        def pair(j, _):
            wide = []
            for e in range(2):
                k = o * per + 2 * j + e
                c = jnp.bitwise_xor(k, mask_ref[o * per // half])
                wide.append(adj[pl.ds(pl.multiple_of(c * tall, 8), tall), :])
            ah, al = split(jnp.concatenate(wide, axis=1))
            ih, il = ih_ref[...], il_ref[...]
            value = dot(ih, ah) + (dot(il, ah) + dot(ih, al))
            out[2 * j] = value[:, :par_dev]
            out[2 * j + 1] = value[:, par_dev:]
            return 0

        lax.fori_loop(0, per // 2, pair, 0)


def forward_kernel(packing, mask_ref, th_ref, tl_ref, ih_ref, il_ref, *rest):
    (keep_ref, send_ref, sr_ref, si_ref, sems, whole_ref, field, pred, left) = rest[-9:]
    sr_hbm, si_hbm = rest[-11:-9]
    pieces = rest[:-11]
    cols = packing.cols
    bins, sens_dev, par_dev = sr_ref.shape
    chunks = sems.shape[1]
    block = bins // chunks
    padded = pred.shape[1] // cols // 2
    tall = 2 * padded
    half = cols // 2
    full, width = packing.full, packing.full * LANES
    start_all((sr_hbm, si_hbm), (sr_ref, si_ref), sems, chunks, block)

    per = cols // len(pieces)
    for p, piece in enumerate(pieces):
        for e in range(per):
            k = p * per + e
            whole_ref[jnp.bitwise_xor(k, mask_ref[k // half])] = piece[e]
    for row in list(range(bins, padded)) + list(range(padded + bins, tall)):
        for f in range(pred.shape[0]):
            pred[f, pl.ds(row, cols, stride=tall), :] = jnp.zeros((cols, LANES), F32)

    def transform(j, _):
        ah, al = split(jnp.concatenate([whole_ref[2 * j], whole_ref[2 * j + 1]], axis=1))
        th, tl = th_ref[...], tl_ref[...]
        value = dot(th, ah) + (dot(tl, ah) + dot(th, al))
        for e in range(2):
            c = 2 * j + e
            part = value[:, e * par_dev : (e + 1) * par_dev]
            field[pl.ds(c, bins, stride=2 * cols), :] = part[:bins]
            field[pl.ds(cols + c, bins, stride=2 * cols), :] = part[padded : padded + bins]
        return 0

    lax.fori_loop(0, cols // 2, transform, 0)

    def chunk_body(chunk, _):
        for copy in spec_copies((sr_hbm, si_hbm), (sr_ref, si_ref), sems, chunk, block):
            copy.wait()
        for i in range(block):
            w = chunk * block + i
            x = field[pl.ds(pl.multiple_of(w * 2 * cols, 8), 2 * cols), :]
            turned = jnp.concatenate([-x[cols:], x[:cols]], axis=0)
            xh, xl = split(jnp.concatenate([x, turned], axis=1))
            sh, sl = split(jnp.concatenate([sr_ref[w], si_ref[w]], axis=1))
            both = dot_nt(jnp.concatenate([xh, xl], axis=0), sh)
            value = both[: 2 * cols] + both[2 * cols :] + dot_nt(xh, sl)
            for f, tile in enumerate(lane_tiles(value)):
                pred[f, pl.ds(w, cols, stride=tall), :] = tile[:cols]
                pred[f, pl.ds(padded + w, cols, stride=tall), :] = tile[cols:]
        return 0

    lax.fori_loop(0, chunks, chunk_body, 0)

    rows = packing.rows
    count = ih_ref.shape[0] // 2
    for c in range(cols):
        wide = [pred[f, c * tall : (c + 1) * tall, :] for f in range(pred.shape[0])]
        ph, pl_low = split(jnp.concatenate(wide, axis=1))
        ih, il = ih_ref[...], il_ref[...]
        value = dot(ih, ph) + (dot(il, ph) + dot(ih, pl_low))
        for f in range(full):
            part = value[:, f * LANES : (f + 1) * LANES]
            keep_ref[pl.ds(c * full + f, count, stride=rows), :] = part[:count]
            send_ref[pl.ds(c * full + f, count, stride=rows), :] = part[count:]
        if packing.rest:
            place = c % packing.share
            part = value[:, width:]
            if place:
                part = pltpu.roll(part, place * packing.rest, 1)
                left[...] += part
            else:
                left[...] = part
            if place == packing.share - 1 or c == cols - 1:
                row = cols * full + c // packing.share
                keep_ref[pl.ds(row, count, stride=rows), :] = left[:count]
                send_ref[pl.ds(row, count, stride=rows), :] = left[count:]


def prepare_kernel(packing, index_ref, map_ref, prior_ref, fh_ref, fl_ref, inv_ref, rows_ref,
                   oh_ref, ol_ref, th_ref, tl_ref, ih_ref, il_ref, select, table):
    step = pl.program_id(0)
    blocks = oh_ref.shape[2] // packing.width
    times = inv_ref.shape[1]

    @pl.when(step == 0)
    def _():
        lane = lax.broadcasted_iota(jnp.int32, (1, packing.width), 1)
        width = packing.full * LANES
        if packing.rest:
            beyond = lane - width
            folded = width + lax.rem(jnp.maximum(beyond, 0), packing.rest)
            local = jnp.where(beyond >= 0, folded, lane)
            valid = beyond < packing.share * packing.rest
        else:
            local = lane
            valid = lane >= 0
        for m in range(blocks):
            owner = jnp.bitwise_xor(index_ref[0], m)
            wanted = jnp.where(valid, owner * packing.sens_dev + local, -1)
            hit = map_ref[...] == wanted
            select[:, m * packing.width : (m + 1) * packing.width] = jnp.where(hit, 1.0, 0.0).astype(BF16)
        ph, pl_low = split(prior_ref[...])
        folded_table = dot_nt(fh_ref[...], ph) + (dot_nt(fl_ref[...], ph) + dot_nt(fh_ref[...], pl_low))
        th, tl = split(folded_table)
        th_ref[...] = th
        tl_ref[...] = tl
        par = inv_ref.shape[0]
        pairs = par // 2
        for r in range(2):
            for d in range(pairs):
                z = lax.rem(index_ref[1] // 2 + d, pairs)
                core = jnp.bitwise_xor(lax.rem(index_ref[1], 2), r)
                j = r * pairs + d
                table[j * times : (j + 1) * times, :] = inv_ref[2 * z + core]
        ih, il = split(table[...])
        ih_ref[...] = ih
        il_ref[...] = il

    group, count, sensors = rows_ref.shape
    high, low = split(rows_ref[...].reshape(group * count, sensors))
    moved = dot(jnp.concatenate([high, low], axis=0), select[...]).astype(BF16)
    oh_ref[...] = moved[: group * count].reshape(oh_ref.shape)
    ol_ref[...] = moved[group * count :].reshape(ol_ref.shape)


def update_kernel(packing, oh_hbm, ol_hbm, *rest):
    gathered, (out_ref, oh_ref, ol_ref, sems) = rest[:-4], rest[-4:]
    times = oh_ref.shape[0]
    chunks = sems.shape[1]
    start_all((oh_hbm, ol_hbm), (oh_ref, ol_ref), sems, chunks, times // chunks)
    cols, rows, full = packing.cols, packing.rows, packing.full
    total = jnp.zeros(out_ref.shape, F32)
    if packing.rest:
        row = lax.broadcasted_iota(jnp.int32, (cols, LANES), 0)
        lane = lax.broadcasted_iota(jnp.int32, (cols, LANES), 1)
        own = lax.rem(row, packing.share) == lane // packing.rest
        shared = row // packing.share

    group = times // chunks

    def body(i, total):
        for copy in spec_copies((oh_hbm, ol_hbm), (oh_ref, ol_ref), sems, i, group):
            copy.wait()
        base = i * (group * rows)
        if group * rows % 8 == 0:
            base = pl.multiple_of(base, 8)
        for m, ref in enumerate(gathered):
            block = ref[pl.ds(base, group * rows), :]
            place = slice(m * packing.width, (m + 1) * packing.width)
            for g in range(group):
                held = block[g * rows : (g + 1) * rows]
                parts = []
                if full == 1:
                    parts.append(held[:cols])
                elif full > 1:
                    wide = held[: cols * full].reshape(cols, full, LANES)
                    parts.extend(wide[:, f, :] for f in range(full))
                if packing.rest:
                    spread = jnp.zeros((cols, LANES), F32)
                    for j in range(packing.rest_rows):
                        line = held[cols * full + j : cols * full + j + 1]
                        spread = jnp.where(own & (shared == j), line, spread)
                    parts.append(spread)
                xh, xl = split(jnp.concatenate(parts, axis=1))
                t = i * group + g
                both = dot_nt(jnp.concatenate([xh, xl], axis=0), oh_ref[t, :, place])
                total = total + (both[:cols] + both[cols:] + dot_nt(xh, ol_ref[t, :, place]))
        return total

    out_ref[...] = lax.fori_loop(0, chunks, body, total)


def whole(array):
    return pl.BlockSpec(array.shape, lambda *_: (0,) * array.ndim)


def swap(size, mask):
    return [(k, k ^ mask) for k in range(size)]


def reduce_quarters(keep, send, first, second, size):
    near = keep + lax.ppermute(send, "sens", swap(size, first))
    return near


def reduce_rest(near, first, second, size):
    per = near.shape[0] // 2
    here = near[:per] + lax.ppermute(near[per:], "sens", swap(size, second))
    over = lax.ppermute(here, "sens", swap(size, second))
    back = lax.ppermute(here, "sens", swap(size, first))
    return [here, over, back, lax.ppermute(over, "sens", swap(size, first))]


def shards(records, spec_real, spec_imag, prior_cov, sensor_map, inverse_rows):
    cols, sens_dev, steps = records.shape
    bins, _, par_dev = spec_real.shape
    padded = round_up(bins, 8)
    sens, par = lax.axis_size("sens"), lax.axis_size("par")
    sens_index, par_index = lax.axis_index("sens"), lax.axis_index("par")
    packing = Packing(cols, sens_dev)
    rows_dev, times, sensors = inverse_rows.shape
    quarters = sens == 4 and cols % 8 == 0
    limit = 58 * 2**20

    fwd = forward_table(steps, bins, padded)
    inv = inverse_table(steps, bins, padded)
    fh, fl = (jnp.asarray(part) for part in split_host(fwd))
    ih, il = (jnp.asarray(part) for part in split_host(inv))
    inv_blocks = jnp.asarray(inv.reshape(par, times, 2 * padded).astype(np.float32))

    if quarters:
        bit0, bit1 = sens_index & 1, sens_index >> 1
        unit = cols // 8
        mask = jnp.stack([(2 * bit0 + bit1) * unit, (2 * bit1 + bit0) * unit]).astype(jnp.int32)
        n_out = 4
    else:
        mask = jnp.zeros((2,), jnp.int32)
        n_out = 1

    by_sensor = jnp.transpose(records, (1, 0, 2))
    by_time = jnp.transpose(inverse_rows, (1, 0, 2))
    block = block_of(bins, 15)
    outside = pl.BlockSpec(memory_space=pltpu.HBM)
    spec_scratch = [
        pltpu.VMEM(spec_real.shape, F32),
        pltpu.VMEM(spec_real.shape, F32),
        pltpu.SemaphoreType.DMA((2, bins // block)),
    ]
    sens_tiles = -(-sens_dev // LANES)
    smem = pl.BlockSpec(memory_space=pltpu.SMEM)
    phase_cost = pl.CostEstimate(
        flops=24 * cols * bins * sens_dev * par_dev, bytes_accessed=8 * bins * sens_dev * par_dev, transcendentals=0
    )
    out_a = [jax.ShapeDtypeStruct((cols // n_out, steps, par_dev), F32)] * n_out
    parts = pl.pallas_call(
        adjoint_kernel,
        in_specs=[smem, whole(by_sensor), whole(fh), whole(fl), whole(ih), whole(il), outside, outside],
        out_specs=[whole(shape) for shape in out_a],
        out_shape=out_a,
        scratch_shapes=spec_scratch
        + [
            pltpu.VMEM((-(-steps // LANES), sens_dev * cols, LANES), F32),
            pltpu.VMEM((sens_tiles, bins * 2 * cols, LANES), F32),
            pltpu.VMEM((cols * 2 * padded, par_dev), F32),
        ],
        compiler_params=pltpu.CompilerParams(vmem_limit_bytes=limit),
        cost_estimate=phase_cost,
        name="adjoint",
    )(mask, by_sensor, fh, fl, ih, il, spec_real, spec_imag)

    index = jnp.stack([sens_index, par_index]).astype(jnp.int32)
    *parts, index = lax.optimization_barrier((*parts, index))
    time_block = block_of(times, 4)
    width = sens * packing.width
    moved = jax.ShapeDtypeStruct((times, rows_dev, width), BF16)
    folded = jax.ShapeDtypeStruct((2 * padded, steps), BF16)
    turned = jax.ShapeDtypeStruct((steps, 2 * padded), BF16)
    map_column = sensor_map.reshape(sensors, 1)
    oh, ol, th, tl, ih2, il2 = pl.pallas_call(
        functools.partial(prepare_kernel, packing),
        grid=(times // time_block,),
        in_specs=[
            smem,
            whole(map_column),
            whole(prior_cov),
            whole(fh),
            whole(fl),
            whole(inv_blocks),
            pl.BlockSpec((time_block, rows_dev, sensors), lambda i: (i, 0, 0)),
        ],
        out_specs=[pl.BlockSpec((time_block, rows_dev, width), lambda i: (i, 0, 0))] * 2
        + [whole(folded)] * 2
        + [whole(turned)] * 2,
        out_shape=[moved, moved, folded, folded, turned, turned],
        scratch_shapes=[pltpu.VMEM((sensors, width), BF16), pltpu.VMEM((steps, 2 * padded), F32)],
        compiler_params=pltpu.CompilerParams(vmem_limit_bytes=limit),
        cost_estimate=pl.CostEstimate(
            flops=4 * rows_dev * times * sensors * width, bytes_accessed=8 * rows_dev * times * sensors, transcendentals=0
        ),
        name="prepare",
    )(index, map_column, prior_cov, fh, fl, inv_blocks, by_time)

    if quarters:
        near0 = reduce_quarters(parts[0], parts[1], 1, 2, sens)
        near1 = reduce_quarters(parts[2], parts[3], 2, 1, sens)
        near0, near1, th = lax.optimization_barrier((near0, near1, th))
        pieces = reduce_rest(near0, 1, 2, sens) + reduce_rest(near1, 2, 1, sens)
    else:
        pieces = [lax.psum(parts[0], "sens")]

    shard_rows = times * packing.rows
    half = jax.ShapeDtypeStruct((par // 2 * shard_rows, LANES), F32)
    keep, send = pl.pallas_call(
        functools.partial(forward_kernel, packing),
        in_specs=[smem, whole(th), whole(tl), whole(ih2), whole(il2)]
        + [whole(piece) for piece in pieces]
        + [outside, outside],
        out_specs=[whole(half)] * 2,
        out_shape=[half, half],
        scratch_shapes=spec_scratch
        + [
            pltpu.VMEM((cols, steps, par_dev), F32),
            pltpu.VMEM((bins * 2 * cols, par_dev), F32),
            pltpu.VMEM((sens_tiles, cols * 2 * padded, LANES), F32),
            pltpu.VMEM((steps, LANES), F32),
        ],
        compiler_params=pltpu.CompilerParams(vmem_limit_bytes=limit),
        cost_estimate=phase_cost,
        name="forward",
    )(mask, th, tl, ih2, il2, *pieces, spec_real, spec_imag)

    pair = keep + lax.ppermute(send, "par", swap(par, 1))
    mine = pair[:shard_rows]
    for d in range(1, par // 2):
        there = pair[d * shard_rows : (d + 1) * shard_rows]
        mine = mine + lax.ppermute(there, "par", [(k, (k + 2 * d) % par) for k in range(par)])
    gathered = [mine] + [lax.ppermute(mine, "sens", swap(sens, m)) for m in range(1, sens)]

    result = jax.ShapeDtypeStruct((cols, rows_dev), F32)
    partial = pl.pallas_call(
        functools.partial(update_kernel, packing),
        in_specs=[outside, outside] + [whole(part) for part in gathered],
        out_shape=result,
        scratch_shapes=[
            pltpu.VMEM(oh.shape, BF16),
            pltpu.VMEM(ol.shape, BF16),
            pltpu.SemaphoreType.DMA((2, times // block_of(times, 2))),
        ],
        compiler_params=pltpu.CompilerParams(vmem_limit_bytes=limit),
        cost_estimate=pl.CostEstimate(
            flops=6 * rows_dev * times * cols * width, bytes_accessed=4 * rows_dev * times * width, transcendentals=0
        ),
        name="update",
    )(oh, ol, *gathered)
    per_dev = cols // par
    spread = lax.all_to_all(partial.reshape(par, per_dev, rows_dev), "par", 0, 0)
    return jnp.sum(spread, axis=0)


def solution(mesh):
    return jax.shard_map(
        shards,
        mesh=mesh,
        in_specs=(
            P(None, "sens", None),
            P(None, "sens", "par"),
            P(None, "sens", "par"),
            P(),
            P(),
            P("sens", "par", None),
        ),
        out_specs=P("par", "sens"),
        check_vma=False,
    )
```

```python
import functools

import jax
import jax.numpy as jnp
import numpy as np
from jax import lax
from jax.experimental import pallas as pl
from jax.experimental.pallas import tpu as pltpu
from jax.sharding import PartitionSpec as P

F32 = jnp.float32
BF16 = jnp.bfloat16
LANES = 128


def round_up(value, step):
    return (value + step - 1) // step * step


def split(value):
    high = value.astype(BF16)
    low = (value - high.astype(F32)).astype(BF16)
    return high, low


def dot(left, right):
    return lax.dot_general(left, right, (((1,), (0,)), ((), ())), preferred_element_type=F32)


def dot_nt(left, right):
    return lax.dot_general(left, right, (((1,), (1,)), ((), ())), preferred_element_type=F32)


def split_host(table):
    high = table.astype(np.float32).astype(jnp.bfloat16)
    low = (table - high.astype(np.float64)).astype(jnp.bfloat16)
    return high, low


def forward_table(steps, bins, padded):
    length = 2 * steps
    phase = 2.0 * np.pi * ((np.arange(bins)[:, None] * np.arange(steps)[None, :]) % length) / length
    table = np.zeros((2 * padded, steps))
    table[:bins] = np.cos(phase)
    table[padded : padded + bins] = -np.sin(phase)
    return table


def inverse_table(steps, bins, padded):
    length = 2 * steps
    phase = 2.0 * np.pi * ((np.arange(steps)[:, None] * np.arange(bins)[None, :]) % length) / length
    weight = np.full((bins,), 2.0)
    weight[0] = 1.0
    weight[-1] = 1.0
    weight = weight / length
    table = np.zeros((steps, 2 * padded))
    table[:, :bins] = np.cos(phase) * weight
    table[:, padded : padded + bins] = -np.sin(phase) * weight
    return table


def block_of(bins, most):
    return max(size for size in range(1, most + 1) if bins % size == 0)


class Packing:
    def __init__(self, cols, sens_dev):
        self.cols = cols
        self.sens_dev = sens_dev
        self.full = sens_dev // LANES
        self.rest = sens_dev % LANES
        self.share = LANES // self.rest if self.rest else 1
        self.rest_rows = -(-cols // self.share) if self.rest else 0
        self.rows = self.full * cols + self.rest_rows
        self.width = LANES * (self.full + (1 if self.rest else 0))


def lane_tiles(value):
    rows, columns = value.shape
    tiles = []
    for start in range(0, columns, LANES):
        tile = value[:, start : start + LANES]
        short = LANES - tile.shape[1]
        if short:
            tile = jnp.concatenate([tile, jnp.zeros((rows, short), value.dtype)], axis=1)
        tiles.append(tile)
    return tiles


def spec_copies(hbm_refs, vmem_refs, sems, chunk, block):
    part = pl.ds(chunk * block, block)
    return [
        pltpu.make_async_copy(hbm.at[part], vmem.at[part], sems.at[j, chunk])
        for j, (hbm, vmem) in enumerate(zip(hbm_refs, vmem_refs))
    ]


def start_all(hbm_refs, vmem_refs, sems, chunks, block):
    for chunk in range(chunks):
        for copy in spec_copies(hbm_refs, vmem_refs, sems, chunk, block):
            copy.start()


def adjoint_kernel(mask_ref, rec_ref, fh_ref, fl_ref, ih_ref, il_ref, sr_hbm, si_hbm, *rest):
    outs, (sr_ref, si_ref, sems, spread, rec_spec, adj) = rest[:-6], rest[-6:]
    sens_dev, cols, steps = rec_ref.shape
    bins, _, par_dev = sr_ref.shape
    chunks = sems.shape[1]
    block = bins // chunks
    padded = adj.shape[0] // cols // 2
    tall = 2 * padded
    half = cols // 2
    start_all((sr_hbm, si_hbm), (sr_ref, si_ref), sems, chunks, block)

    every = rec_ref[...].reshape(sens_dev * cols, steps)
    for f, tile in enumerate(lane_tiles(every)):
        spread[f] = tile
    for row in list(range(bins, padded)) + list(range(padded + bins, tall)):
        adj[pl.ds(row, cols, stride=tall), :] = jnp.zeros((cols, par_dev), F32)

    def column(c, _):
        own = [spread[f, pl.ds(c, sens_dev, stride=cols), :] for f in range(spread.shape[0])]
        rh, rl = split(jnp.concatenate(own, axis=1)[:, :steps])
        fh, fl = fh_ref[...], fl_ref[...]
        value = dot_nt(fh, rh) + (dot_nt(fl, rh) + dot_nt(fh, rl))
        for f, tile in enumerate(lane_tiles(value)):
            rec_spec[f, pl.ds(c, bins, stride=2 * cols), :] = tile[:bins]
            rec_spec[f, pl.ds(cols + c, bins, stride=2 * cols), :] = tile[padded : padded + bins]
        return 0

    lax.fori_loop(0, cols, column, 0, unroll=4)

    def chunk_body(chunk, _):
        for copy in spec_copies((sr_hbm, si_hbm), (sr_ref, si_ref), sems, chunk, block):
            copy.wait()
        for i in range(block):
            w = chunk * block + i
            at = pl.ds(pl.multiple_of(w * 2 * cols, 8), 2 * cols)
            x = jnp.concatenate([rec_spec[f, at, :] for f in range(rec_spec.shape[0])], axis=1)[:, :sens_dev]
            xh, xl = split(x)
            sh, sl = split(jnp.concatenate([sr_ref[w], si_ref[w]], axis=1))
            both = dot(jnp.concatenate([xh, xl], axis=0), sh)
            value = both[: 2 * cols] + both[2 * cols :] + dot(xh, sl)
            adj[pl.ds(w, cols, stride=tall), :] = value[:cols, :par_dev] + value[cols:, par_dev:]
            adj[pl.ds(padded + w, cols, stride=tall), :] = value[cols:, :par_dev] - value[:cols, par_dev:]
        return 0

    lax.fori_loop(0, chunks, chunk_body, 0)

    per = cols // len(outs)
    for o, out in enumerate(outs):
        def pair(j, _):
            wide = []
            for e in range(2):
                k = o * per + 2 * j + e
                c = jnp.bitwise_xor(k, mask_ref[o * per // half])
                wide.append(adj[pl.ds(pl.multiple_of(c * tall, 8), tall), :])
            ah, al = split(jnp.concatenate(wide, axis=1))
            ih, il = ih_ref[...], il_ref[...]
            value = dot(ih, ah) + (dot(il, ah) + dot(ih, al))
            out[2 * j] = value[:, :par_dev]
            out[2 * j + 1] = value[:, par_dev:]
            return 0

        lax.fori_loop(0, per // 2, pair, 0, unroll=True)


def forward_kernel(packing, mask_ref, th_ref, tl_ref, ih_ref, il_ref, *rest):
    keep_refs, send_refs = rest[-11:-9], rest[-9:-7]
    (sr_ref, si_ref, sems, whole_ref, field, pred, left) = rest[-7:]
    sr_hbm, si_hbm = rest[-13:-11]
    pieces = rest[:-13]
    cols = 2 * packing.cols
    bins, sens_dev, par_dev = sr_ref.shape
    chunks = sems.shape[1]
    block = bins // chunks
    padded = pred.shape[1] // cols // 2
    tall = 2 * padded
    half = cols // 2
    full, width = packing.full, packing.full * LANES
    start_all((sr_hbm, si_hbm), (sr_ref, si_ref), sems, chunks, block)

    per = cols // len(pieces)
    for p, piece in enumerate(pieces):
        for e in range(per):
            k = p * per + e
            whole_ref[jnp.bitwise_xor(k, mask_ref[k // half])] = piece[e]
    for row in list(range(bins, padded)) + list(range(padded + bins, tall)):
        for f in range(pred.shape[0]):
            pred[f, pl.ds(row, cols, stride=tall), :] = jnp.zeros((cols, LANES), F32)

    def transform(j, _):
        ah, al = split(jnp.concatenate([whole_ref[2 * j], whole_ref[2 * j + 1]], axis=1))
        th, tl = th_ref[...], tl_ref[...]
        value = dot(th, ah) + (dot(tl, ah) + dot(th, al))
        for e in range(2):
            c = 2 * j + e
            part = value[:, e * par_dev : (e + 1) * par_dev]
            field[pl.ds(c, bins, stride=2 * cols), :] = part[:bins]
            field[pl.ds(cols + c, bins, stride=2 * cols), :] = part[padded : padded + bins]
        return 0

    lax.fori_loop(0, cols // 2, transform, 0, unroll=4)

    def chunk_body(chunk, _):
        for copy in spec_copies((sr_hbm, si_hbm), (sr_ref, si_ref), sems, chunk, block):
            copy.wait()
        for i in range(block):
            w = chunk * block + i
            x = field[pl.ds(pl.multiple_of(w * 2 * cols, 8), 2 * cols), :]
            turned = jnp.concatenate([-x[cols:], x[:cols]], axis=0)
            xh, xl = split(jnp.concatenate([x, turned], axis=1))
            sh, sl = split(jnp.concatenate([sr_ref[w], si_ref[w]], axis=1))
            both = dot_nt(jnp.concatenate([xh, xl], axis=0), sh)
            value = both[: 2 * cols] + both[2 * cols :] + dot_nt(xh, sl)
            for f, tile in enumerate(lane_tiles(value)):
                pred[f, pl.ds(w, cols, stride=tall), :] = tile[:cols]
                pred[f, pl.ds(padded + w, cols, stride=tall), :] = tile[cols:]
        return 0

    lax.fori_loop(0, chunks, chunk_body, 0)

    rows = packing.rows
    count = ih_ref.shape[0] // 2
    for column in range(cols):
        keep_ref, send_ref = keep_refs[column // packing.cols], send_refs[column // packing.cols]
        c = column % packing.cols
        wide = [pred[f, column * tall : (column + 1) * tall, :] for f in range(pred.shape[0])]
        ph, pl_low = split(jnp.concatenate(wide, axis=1))
        ih, il = ih_ref[...], il_ref[...]
        value = dot(ih, ph) + (dot(il, ph) + dot(ih, pl_low))
        for f in range(full):
            part = value[:, f * LANES : (f + 1) * LANES]
            keep_ref[pl.ds(c * full + f, count, stride=rows), :] = part[:count]
            send_ref[pl.ds(c * full + f, count, stride=rows), :] = part[count:]
        if packing.rest:
            place = c % packing.share
            part = value[:, width:]
            if place:
                part = pltpu.roll(part, place * packing.rest, 1)
                left[...] += part
            else:
                left[...] = part
            if place == packing.share - 1 or c == packing.cols - 1:
                row = packing.cols * full + c // packing.share
                keep_ref[pl.ds(row, count, stride=rows), :] = left[:count]
                send_ref[pl.ds(row, count, stride=rows), :] = left[count:]


def tables_kernel(packing, index_ref, map_ref, prior_ref, fh_ref, fl_ref, inv_ref,
                  select, th_ref, tl_ref, ih_ref, il_ref, table):
    blocks = select.shape[1] // packing.width
    times = inv_ref.shape[1]
    lane = lax.broadcasted_iota(jnp.int32, (1, packing.width), 1)
    width = packing.full * LANES
    if packing.rest:
        beyond = lane - width
        folded = width + lax.rem(jnp.maximum(beyond, 0), packing.rest)
        local = jnp.where(beyond >= 0, folded, lane)
        valid = beyond < packing.share * packing.rest
    else:
        local = lane
        valid = lane >= 0
    for m in range(blocks):
        owner = jnp.bitwise_xor(index_ref[0], m)
        wanted = jnp.where(valid, owner * packing.sens_dev + local, -1)
        hit = map_ref[...] == wanted
        select[:, m * packing.width : (m + 1) * packing.width] = jnp.where(hit, 1.0, 0.0).astype(BF16)
    ph, pl_low = split(prior_ref[...])
    folded_table = dot_nt(fh_ref[...], ph) + (dot_nt(fl_ref[...], ph) + dot_nt(fh_ref[...], pl_low))
    th, tl = split(folded_table)
    th_ref[...] = th
    tl_ref[...] = tl
    par = inv_ref.shape[0]
    pairs = par // 2
    for r in range(2):
        for d in range(pairs):
            z = lax.rem(index_ref[1] // 2 + d, pairs)
            core = jnp.bitwise_xor(lax.rem(index_ref[1], 2), r)
            j = r * pairs + d
            table[j * times : (j + 1) * times, :] = inv_ref[2 * z + core]
    ih, il = split(table[...])
    ih_ref[...] = ih
    il_ref[...] = il


def rows_kernel(select, rows_ref, oh_ref, ol_ref):
    group, count, sensors = rows_ref.shape
    high, low = split(rows_ref[...].reshape(group * count, sensors))
    moved = dot(jnp.concatenate([high, low], axis=0), select[...]).astype(BF16)
    oh_ref[...] = moved[: group * count].reshape(oh_ref.shape)
    ol_ref[...] = moved[group * count :].reshape(ol_ref.shape)


def update_kernel(packing, count, *rest):
    high, low, gathered = rest[:count], rest[count : 2 * count], rest[2 * count : -4]
    out_ref, oh_ref, ol_ref, sems = rest[-4:]
    times = oh_ref.shape[0]
    chunks = sems.shape[1]
    group = times // chunks
    sources, first = [], 0
    for hbm in zip(high, low):
        part = pl.ds(first * group, hbm[0].shape[0])
        own_chunks = hbm[0].shape[0] // group
        held = (hbm, (oh_ref.at[part], ol_ref.at[part]), sems.at[:, pl.ds(first, own_chunks)])
        start_all(*held, own_chunks, group)
        sources.append((first, own_chunks, held))
        first += own_chunks
    cols, rows, full = packing.cols, packing.rows, packing.full
    sens = len(gathered) // 2
    if packing.rest:
        row = lax.broadcasted_iota(jnp.int32, (cols, LANES), 0)
        lane = lax.broadcasted_iota(jnp.int32, (cols, LANES), 1)
        own = lax.rem(row, packing.share) == lane // packing.rest
        shared = row // packing.share

    def unpack(held):
        parts = []
        if full == 1:
            parts.append(held[:cols])
        elif full > 1:
            wide = held[: cols * full].reshape(cols, full, LANES)
            parts.extend(wide[:, f, :] for f in range(full))
        if packing.rest:
            spread = jnp.zeros((cols, LANES), F32)
            for j in range(packing.rest_rows):
                line = held[cols * full + j : cols * full + j + 1]
                spread = jnp.where(own & (shared == j), line, spread)
            parts.append(spread)
        return jnp.concatenate(parts, axis=1)

    def body(first, held, step, total):
        i = first + step
        for copy in spec_copies(*held, step, group):
            copy.wait()
        base = i * (group * rows)
        if group * rows % 8 == 0:
            base = pl.multiple_of(base, 8)
        for m in range(sens):
            blocks = [gathered[h * sens + m][pl.ds(base, group * rows), :] for h in range(2)]
            place = slice(m * packing.width, (m + 1) * packing.width)
            for g in range(group):
                x = jnp.concatenate([unpack(block[g * rows : (g + 1) * rows]) for block in blocks], axis=0)
                xh, xl = split(x)
                t = i * group + g
                both = dot_nt(jnp.concatenate([xh, xl], axis=0), oh_ref[t, :, place])
                total = total + (both[: 2 * cols] + both[2 * cols :] + dot_nt(xh, ol_ref[t, :, place]))
        return total

    total = jnp.zeros(out_ref.shape, F32)
    for first, own_chunks, held in sources:
        total = lax.fori_loop(0, own_chunks, functools.partial(body, first, held), total)
    out_ref[...] = total


def whole(array):
    return pl.BlockSpec(array.shape, lambda *_: (0,) * array.ndim)


def swap(size, mask):
    return [(k, k ^ mask) for k in range(size)]


def reduce_near(keep, send, first, size):
    return keep + lax.ppermute(send, "sens", swap(size, first))


def reduce_here(near, second, size):
    per = near.shape[0] // 2
    return near[:per] + lax.ppermute(near[per:], "sens", swap(size, second))


def spread_back(here, first, second, size):
    over = lax.ppermute(here, "sens", swap(size, second))
    back = lax.ppermute(here, "sens", swap(size, first))
    return [here, over, back, lax.ppermute(over, "sens", swap(size, first))]


def shards(records, spec_real, spec_imag, prior_cov, sensor_map, inverse_rows):
    cols, sens_dev, steps = records.shape
    bins, _, par_dev = spec_real.shape
    padded = round_up(bins, 8)
    sens, par = lax.axis_size("sens"), lax.axis_size("par")
    sens_index, par_index = lax.axis_index("sens"), lax.axis_index("par")
    packing = Packing(cols // 2, sens_dev)
    rows_dev, times, sensors = inverse_rows.shape
    quarters = sens == 4 and cols % 8 == 0
    limit = 58 * 2**20

    fwd = forward_table(steps, bins, padded)
    inv = inverse_table(steps, bins, padded)
    fh, fl = (jnp.asarray(part) for part in split_host(fwd))
    ih, il = (jnp.asarray(part) for part in split_host(inv))
    inv_blocks = jnp.asarray(inv.reshape(par, times, 2 * padded).astype(np.float32))

    if quarters:
        bit0, bit1 = sens_index & 1, sens_index >> 1
        unit = cols // 8
        mask = jnp.stack([(2 * bit0 + bit1) * unit, (2 * bit1 + bit0) * unit]).astype(jnp.int32)
        n_out = 4
    else:
        mask = jnp.zeros((2,), jnp.int32)
        n_out = 1

    by_sensor = jnp.transpose(records, (1, 0, 2))
    by_time = jnp.transpose(inverse_rows, (1, 0, 2))
    block = block_of(bins, 15)
    outside = pl.BlockSpec(memory_space=pltpu.HBM)
    spec_scratch = [
        pltpu.VMEM(spec_real.shape, F32),
        pltpu.VMEM(spec_real.shape, F32),
        pltpu.SemaphoreType.DMA((2, bins // block)),
    ]
    sens_tiles = -(-sens_dev // LANES)
    smem = pl.BlockSpec(memory_space=pltpu.SMEM)
    phase_cost = pl.CostEstimate(
        flops=24 * cols * bins * sens_dev * par_dev, bytes_accessed=8 * bins * sens_dev * par_dev, transcendentals=0
    )
    out_a = [jax.ShapeDtypeStruct((cols // n_out, steps, par_dev), F32)] * n_out
    parts = pl.pallas_call(
        adjoint_kernel,
        in_specs=[smem, whole(by_sensor), whole(fh), whole(fl), whole(ih), whole(il), outside, outside],
        out_specs=[whole(shape) for shape in out_a],
        out_shape=out_a,
        scratch_shapes=spec_scratch
        + [
            pltpu.VMEM((-(-steps // LANES), sens_dev * cols, LANES), F32),
            pltpu.VMEM((sens_tiles, bins * 2 * cols, LANES), F32),
            pltpu.VMEM((cols * 2 * padded, par_dev), F32),
        ],
        compiler_params=pltpu.CompilerParams(vmem_limit_bytes=limit),
        cost_estimate=phase_cost,
        name="adjoint",
    )(mask, by_sensor, fh, fl, ih, il, spec_real, spec_imag)

    index = jnp.stack([sens_index, par_index]).astype(jnp.int32)
    *parts, index = lax.optimization_barrier((*parts, index))
    time_block = block_of(times, 4)
    width = sens * packing.width
    moved = jax.ShapeDtypeStruct((times, rows_dev, width), BF16)
    folded = jax.ShapeDtypeStruct((2 * padded, steps), BF16)
    turned = jax.ShapeDtypeStruct((steps, 2 * padded), BF16)
    map_column = sensor_map.reshape(sensors, 1)
    chosen = jax.ShapeDtypeStruct((sensors, width), BF16)
    select, th, tl, ih2, il2 = pl.pallas_call(
        functools.partial(tables_kernel, packing),
        in_specs=[smem, whole(map_column), whole(prior_cov), whole(fh), whole(fl), whole(inv_blocks)],
        out_shape=[chosen, folded, folded, turned, turned],
        scratch_shapes=[pltpu.VMEM((steps, 2 * padded), F32)],
        compiler_params=pltpu.CompilerParams(vmem_limit_bytes=limit),
        name="tables",
    )(index, map_column, prior_cov, fh, fl, inv_blocks)

    blocks = times // time_block
    third = max(blocks // 3, 1)
    cuts = [0, third, 2 * third, blocks] if blocks >= 3 else [0, blocks]

    def move_rows(number, chosen_rows):
        start, stop = cuts[number], cuts[number + 1]
        moved = jax.ShapeDtypeStruct(((stop - start) * time_block, rows_dev, width), BF16)
        return pl.pallas_call(
            rows_kernel,
            grid=(stop - start,),
            in_specs=[
                whole(chosen),
                pl.BlockSpec((time_block, rows_dev, sensors), lambda i: (i + start, 0, 0)),
            ],
            out_specs=[pl.BlockSpec((time_block, rows_dev, width), lambda i: (i, 0, 0))] * 2,
            out_shape=[moved, moved],
            compiler_params=pltpu.CompilerParams(vmem_limit_bytes=limit),
            cost_estimate=pl.CostEstimate(
                flops=4 * rows_dev * moved.shape[0] * sensors * width,
                bytes_accessed=8 * rows_dev * moved.shape[0] * sensors,
                transcendentals=0,
            ),
            name="rows",
        )(chosen_rows, by_time)

    ready = [move_rows(0, select)]
    if quarters and len(cuts) == 4:
        near0 = reduce_near(parts[0], parts[1], 1, sens)
        near1 = reduce_near(parts[2], parts[3], 2, sens)
        near0, near1, th, ready[0], select = lax.optimization_barrier((near0, near1, th, ready[0], select))
        ready.append(move_rows(1, select))
        here0, here1 = reduce_here(near0, 2, sens), reduce_here(near1, 1, sens)
        here0, here1, ready[1], select = lax.optimization_barrier((here0, here1, ready[1], select))
        ready.append(move_rows(2, select))
        pieces = spread_back(here0, 1, 2, sens) + spread_back(here1, 2, 1, sens)
        pieces[-1], ready[2] = lax.optimization_barrier((pieces[-1], ready[2]))
    else:
        pieces = [lax.psum(jnp.concatenate(parts, axis=0), "sens")]
        ready.extend(move_rows(number, select) for number in range(1, len(cuts) - 1))

    shard_rows = times * packing.rows
    half = jax.ShapeDtypeStruct((par // 2 * shard_rows, LANES), F32)
    keep0, keep1, send0, send1 = pl.pallas_call(
        functools.partial(forward_kernel, packing),
        in_specs=[smem, whole(th), whole(tl), whole(ih2), whole(il2)]
        + [whole(piece) for piece in pieces]
        + [outside, outside],
        out_specs=[whole(half)] * 4,
        out_shape=[half] * 4,
        scratch_shapes=spec_scratch
        + [
            pltpu.VMEM((cols, steps, par_dev), F32),
            pltpu.VMEM((bins * 2 * cols, par_dev), F32),
            pltpu.VMEM((sens_tiles, cols * 2 * padded, LANES), F32),
            pltpu.VMEM((steps, LANES), F32),
        ],
        compiler_params=pltpu.CompilerParams(vmem_limit_bytes=limit),
        cost_estimate=phase_cost,
        name="forward",
    )(mask, th, tl, ih2, il2, *pieces, spec_real, spec_imag)

    def over_pairs(pair, d):
        there = pair[d * shard_rows : (d + 1) * shard_rows]
        return lax.ppermute(there, "par", [(k, (k + 2 * d) % par) for k in range(par)])

    def over_sens(mine):
        return [mine] + [lax.ppermute(mine, "sens", swap(sens, m)) for m in range(1, sens)]

    pair0 = keep0 + lax.ppermute(send0, "par", swap(par, 1))
    pair1 = keep1 + lax.ppermute(send1, "par", swap(par, 1))
    come = [over_pairs(pair0, d) for d in range(1, par // 2)]
    come[0], come[-1], pair1 = lax.optimization_barrier((come[0], come[-1], pair1))
    mine0 = pair0[:shard_rows] + sum(come[1:], come[0])
    mine1 = pair1[:shard_rows] + sum(over_pairs(pair1, d) for d in range(1, par // 2))
    gathered = over_sens(mine0) + over_sens(mine1)

    result = jax.ShapeDtypeStruct((cols, rows_dev), F32)
    partial = pl.pallas_call(
        functools.partial(update_kernel, packing, len(ready)),
        in_specs=[outside] * (2 * len(ready)) + [whole(part) for part in gathered],
        out_shape=result,
        scratch_shapes=[
            pltpu.VMEM(moved.shape, BF16),
            pltpu.VMEM(moved.shape, BF16),
            pltpu.SemaphoreType.DMA((2, blocks)),
        ],
        compiler_params=pltpu.CompilerParams(vmem_limit_bytes=limit),
        cost_estimate=pl.CostEstimate(
            flops=6 * rows_dev * times * cols * width, bytes_accessed=4 * rows_dev * times * width, transcendentals=0
        ),
        name="update",
    )(*(pair[0] for pair in ready), *(pair[1] for pair in ready), *gathered)
    per_dev = cols // par
    spread = lax.all_to_all(partial.reshape(par, per_dev, rows_dev), "par", 0, 0)
    return jnp.sum(spread, axis=0)


def solution(mesh):
    return jax.shard_map(
        shards,
        mesh=mesh,
        in_specs=(
            P(None, "sens", None),
            P(None, "sens", "par"),
            P(None, "sens", "par"),
            P(),
            P(),
            P("sens", "par", None),
        ),
        out_specs=P("par", "sens"),
        check_vma=False,
    )
```

```python
import functools

import jax
import jax.numpy as jnp
import numpy as np
from jax import lax
from jax.experimental import pallas as pl
from jax.experimental.pallas import tpu as pltpu
from jax.sharding import PartitionSpec as P

F32 = jnp.float32
BF16 = jnp.bfloat16
LANES = 128


def round_up(value, step):
    return (value + step - 1) // step * step


def split(value):
    high = value.astype(BF16)
    low = (value - high.astype(F32)).astype(BF16)
    return high, low


def dot(left, right):
    return lax.dot_general(left, right, (((1,), (0,)), ((), ())), preferred_element_type=F32)


def dot_nt(left, right):
    return lax.dot_general(left, right, (((1,), (1,)), ((), ())), preferred_element_type=F32)


def split_host(table):
    high = table.astype(np.float32).astype(jnp.bfloat16)
    low = (table - high.astype(np.float64)).astype(jnp.bfloat16)
    return high, low


def forward_table(steps, bins, padded):
    length = 2 * steps
    phase = 2.0 * np.pi * ((np.arange(bins)[:, None] * np.arange(steps)[None, :]) % length) / length
    table = np.zeros((2 * padded, steps))
    table[:bins] = np.cos(phase)
    table[padded : padded + bins] = -np.sin(phase)
    return table


def inverse_table(steps, bins, padded):
    length = 2 * steps
    phase = 2.0 * np.pi * ((np.arange(steps)[:, None] * np.arange(bins)[None, :]) % length) / length
    weight = np.full((bins,), 2.0)
    weight[0] = 1.0
    weight[-1] = 1.0
    weight = weight / length
    table = np.zeros((steps, 2 * padded))
    table[:, :bins] = np.cos(phase) * weight
    table[:, padded : padded + bins] = -np.sin(phase) * weight
    return table


def block_of(bins, most):
    return max(size for size in range(1, most + 1) if bins % size == 0)


class Packing:
    def __init__(self, cols, sens_dev):
        self.cols = cols
        self.sens_dev = sens_dev
        self.full = sens_dev // LANES
        self.rest = sens_dev % LANES
        self.share = LANES // self.rest if self.rest else 1
        self.rest_rows = -(-cols // self.share) if self.rest else 0
        self.rows = self.full * cols + self.rest_rows
        self.width = LANES * (self.full + (1 if self.rest else 0))


def lane_tiles(value):
    rows, columns = value.shape
    tiles = []
    for start in range(0, columns, LANES):
        tile = value[:, start : start + LANES]
        short = LANES - tile.shape[1]
        if short:
            tile = jnp.concatenate([tile, jnp.zeros((rows, short), value.dtype)], axis=1)
        tiles.append(tile)
    return tiles


def spec_copies(hbm_refs, vmem_refs, sems, chunk, block):
    part = pl.ds(chunk * block, block)
    return [
        pltpu.make_async_copy(hbm.at[part], vmem.at[part], sems.at[j, chunk])
        for j, (hbm, vmem) in enumerate(zip(hbm_refs, vmem_refs))
    ]


def start_all(hbm_refs, vmem_refs, sems, chunks, block):
    for chunk in range(chunks):
        for copy in spec_copies(hbm_refs, vmem_refs, sems, chunk, block):
            copy.start()


def column_masks(quarters, cols):
    if not quarters:
        return (0, 0)
    index = lax.axis_index("sens")
    bit0, bit1 = index & 1, index >> 1
    unit = cols // 8
    return ((2 * bit0 + bit1) * unit, (2 * bit1 + bit0) * unit)


def adjoint_kernel(quarters, rec_ref, fh_ref, fl_ref, ih_ref, il_ref, sr_hbm, si_hbm, *rest):
    outs, (sr_ref, si_ref, sems, spread, rec_spec, adj) = rest[:-6], rest[-6:]
    sens_dev, cols, steps = rec_ref.shape
    bins, _, par_dev = sr_ref.shape
    chunks = sems.shape[1]
    block = bins // chunks
    padded = adj.shape[0] // cols // 2
    tall = 2 * padded
    half = cols // 2
    masks = column_masks(quarters, cols)
    start_all((sr_hbm, si_hbm), (sr_ref, si_ref), sems, chunks, block)

    every = rec_ref[...].reshape(sens_dev * cols, steps)
    for f, tile in enumerate(lane_tiles(every)):
        spread[f] = tile
    for row in list(range(bins, padded)) + list(range(padded + bins, tall)):
        adj[pl.ds(row, cols, stride=tall), :] = jnp.zeros((cols, par_dev), F32)

    def column(c, _):
        own = [spread[f, pl.ds(c, sens_dev, stride=cols), :] for f in range(spread.shape[0])]
        rh, rl = split(jnp.concatenate(own, axis=1)[:, :steps])
        fh, fl = fh_ref[...], fl_ref[...]
        value = dot_nt(fh, rh) + (dot_nt(fl, rh) + dot_nt(fh, rl))
        for f, tile in enumerate(lane_tiles(value)):
            rec_spec[f, pl.ds(c, bins, stride=2 * cols), :] = tile[:bins]
            rec_spec[f, pl.ds(cols + c, bins, stride=2 * cols), :] = tile[padded : padded + bins]
        return 0

    lax.fori_loop(0, cols, column, 0, unroll=True)

    def chunk_body(chunk, _):
        for copy in spec_copies((sr_hbm, si_hbm), (sr_ref, si_ref), sems, chunk, block):
            copy.wait()
        for i in range(block):
            w = chunk * block + i
            at = pl.ds(pl.multiple_of(w * 2 * cols, 8), 2 * cols)
            x = jnp.concatenate([rec_spec[f, at, :] for f in range(rec_spec.shape[0])], axis=1)[:, :sens_dev]
            xh, xl = split(x)
            sh, sl = split(jnp.concatenate([sr_ref[w], si_ref[w]], axis=1))
            both = dot(jnp.concatenate([xh, xl], axis=0), sh)
            value = both[: 2 * cols] + both[2 * cols :] + dot(xh, sl)
            adj[pl.ds(w, cols, stride=tall), :] = value[:cols, :par_dev] + value[cols:, par_dev:]
            adj[pl.ds(padded + w, cols, stride=tall), :] = value[cols:, :par_dev] - value[:cols, par_dev:]
        return 0

    lax.fori_loop(0, chunks, chunk_body, 0)

    per = cols // len(outs)
    for o, out in enumerate(outs):
        def pair(j, _):
            wide = []
            for e in range(2):
                k = o * per + 2 * j + e
                c = k ^ masks[o * per // half]
                wide.append(adj[pl.ds(pl.multiple_of(c * tall, 8), tall), :])
            ah, al = split(jnp.concatenate(wide, axis=1))
            ih, il = ih_ref[...], il_ref[...]
            value = dot(ih, ah) + (dot(il, ah) + dot(ih, al))
            out[2 * j] = value[:, :par_dev]
            out[2 * j + 1] = value[:, par_dev:]
            return 0

        lax.fori_loop(0, per // 2, pair, 0, unroll=True)


def forward_kernel(packing, quarters, th_ref, tl_ref, ih_ref, il_ref, *rest):
    keep_refs, send_refs = rest[-11:-9], rest[-9:-7]
    (sr_ref, si_ref, sems, whole_ref, field, pred, left) = rest[-7:]
    sr_hbm, si_hbm = rest[-13:-11]
    pieces = rest[:-13]
    cols = 2 * packing.cols
    bins, sens_dev, par_dev = sr_ref.shape
    chunks = sems.shape[1]
    block = bins // chunks
    padded = pred.shape[1] // cols // 2
    tall = 2 * padded
    half = cols // 2
    masks = column_masks(quarters, cols)
    full, width = packing.full, packing.full * LANES
    start_all((sr_hbm, si_hbm), (sr_ref, si_ref), sems, chunks, block)

    per = cols // len(pieces)
    for p, piece in enumerate(pieces):
        for e in range(per):
            k = p * per + e
            whole_ref[k ^ masks[k // half]] = piece[e]
    for row in list(range(bins, padded)) + list(range(padded + bins, tall)):
        for f in range(pred.shape[0]):
            pred[f, pl.ds(row, cols, stride=tall), :] = jnp.zeros((cols, LANES), F32)

    def transform(j, _):
        ah, al = split(jnp.concatenate([whole_ref[2 * j], whole_ref[2 * j + 1]], axis=1))
        th, tl = th_ref[...], tl_ref[...]
        value = dot(th, ah) + (dot(tl, ah) + dot(th, al))
        for e in range(2):
            c = 2 * j + e
            part = value[:, e * par_dev : (e + 1) * par_dev]
            field[pl.ds(c, bins, stride=2 * cols), :] = part[:bins]
            field[pl.ds(cols + c, bins, stride=2 * cols), :] = part[padded : padded + bins]
        return 0

    lax.fori_loop(0, cols // 2, transform, 0, unroll=4)

    def chunk_body(chunk, _):
        for copy in spec_copies((sr_hbm, si_hbm), (sr_ref, si_ref), sems, chunk, block):
            copy.wait()
        for i in range(block):
            w = chunk * block + i
            x = field[pl.ds(pl.multiple_of(w * 2 * cols, 8), 2 * cols), :]
            turned = jnp.concatenate([-x[cols:], x[:cols]], axis=0)
            xh, xl = split(jnp.concatenate([x, turned], axis=1))
            sh, sl = split(jnp.concatenate([sr_ref[w], si_ref[w]], axis=1))
            data = jnp.concatenate(
                [
                    jnp.concatenate([xh, xh], axis=1),
                    jnp.concatenate([xl, jnp.zeros_like(xl)], axis=1),
                ],
                axis=0,
            )
            both = dot_nt(jnp.concatenate([sh, sl], axis=1), data).T
            value = both[: 2 * cols] + both[2 * cols :]
            for f, tile in enumerate(lane_tiles(value)):
                pred[f, pl.ds(w, cols, stride=tall), :] = tile[:cols]
                pred[f, pl.ds(padded + w, cols, stride=tall), :] = tile[cols:]
        return 0

    lax.fori_loop(0, chunks, chunk_body, 0)

    rows = packing.rows
    count = ih_ref.shape[0] // 2
    for column in range(cols):
        keep_ref, send_ref = keep_refs[column // packing.cols], send_refs[column // packing.cols]
        c = column % packing.cols
        wide = [pred[f, column * tall : (column + 1) * tall, :] for f in range(pred.shape[0])]
        ph, pl_low = split(jnp.concatenate(wide, axis=1))
        ih, il = ih_ref[...], il_ref[...]
        value = dot(ih, ph) + (dot(il, ph) + dot(ih, pl_low))
        for f in range(full):
            part = value[:, f * LANES : (f + 1) * LANES]
            keep_ref[pl.ds(c * full + f, count, stride=rows), :] = part[:count]
            send_ref[pl.ds(c * full + f, count, stride=rows), :] = part[count:]
        if packing.rest:
            place = c % packing.share
            part = value[:, width:]
            if place:
                part = pltpu.roll(part, place * packing.rest, 1)
                left[...] += part
            else:
                left[...] = part
            if place == packing.share - 1 or c == packing.cols - 1:
                row = packing.cols * full + c // packing.share
                keep_ref[pl.ds(row, count, stride=rows), :] = left[:count]
                send_ref[pl.ds(row, count, stride=rows), :] = left[count:]


def tables_kernel(packing, map_ref, prior_ref, fh_ref, fl_ref, inv_ref,
                  select, th_ref, tl_ref, ih_ref, il_ref, table):
    blocks = select.shape[1] // packing.width
    times = inv_ref.shape[1]
    lane = lax.broadcasted_iota(jnp.int32, (1, packing.width), 1)
    width = packing.full * LANES
    if packing.rest:
        beyond = lane - width
        folded = width + lax.rem(jnp.maximum(beyond, 0), packing.rest)
        local = jnp.where(beyond >= 0, folded, lane)
        valid = beyond < packing.share * packing.rest
    else:
        local = lane
        valid = lane >= 0
    for m in range(blocks):
        owner = lax.axis_index("sens") ^ m
        wanted = jnp.where(valid, owner * packing.sens_dev + local, -1)
        hit = map_ref[...] == wanted
        select[:, m * packing.width : (m + 1) * packing.width] = jnp.where(hit, 1.0, 0.0).astype(BF16)
    ph, pl_low = split(prior_ref[...])
    folded_table = dot_nt(fh_ref[...], ph) + (dot_nt(fl_ref[...], ph) + dot_nt(fh_ref[...], pl_low))
    th, tl = split(folded_table)
    th_ref[...] = th
    tl_ref[...] = tl
    par = inv_ref.shape[0]
    pairs = par // 2
    place = lax.axis_index("par")
    for r in range(2):
        for d in range(pairs):
            z = lax.rem(place // 2 + d, pairs)
            core = lax.rem(place, 2) ^ r
            j = r * pairs + d
            table[j * times : (j + 1) * times, :] = inv_ref[2 * z + core]
    ih, il = split(table[...])
    ih_ref[...] = ih
    il_ref[...] = il


def rows_kernel(select, rows_ref, oh_ref, ol_ref):
    group, count, sensors = rows_ref.shape
    high, low = split(rows_ref[...].reshape(group * count, sensors))
    moved = dot(jnp.concatenate([high, low], axis=0), select[...]).astype(BF16)
    oh_ref[...] = moved[: group * count].reshape(oh_ref.shape)
    ol_ref[...] = moved[group * count :].reshape(ol_ref.shape)


def update_kernel(packing, count, *rest):
    high, low, gathered = rest[:count], rest[count : 2 * count], rest[2 * count : -4]
    out_ref, oh_ref, ol_ref, sems = rest[-4:]
    times = oh_ref.shape[0]
    chunks = sems.shape[1]
    group = times // chunks
    sources, first = [], 0
    for hbm in zip(high, low):
        part = pl.ds(first * group, hbm[0].shape[0])
        own_chunks = hbm[0].shape[0] // group
        held = (hbm, (oh_ref.at[part], ol_ref.at[part]), sems.at[:, pl.ds(first, own_chunks)])
        start_all(*held, own_chunks, group)
        sources.append((first, own_chunks, held))
        first += own_chunks
    cols, rows, full = packing.cols, packing.rows, packing.full
    sens = len(gathered) // 2
    if packing.rest:
        row = lax.broadcasted_iota(jnp.int32, (cols, LANES), 0)
        lane = lax.broadcasted_iota(jnp.int32, (cols, LANES), 1)
        own = lax.rem(row, packing.share) == lane // packing.rest
        shared = row // packing.share

    def unpack(held):
        parts = []
        if full == 1:
            parts.append(held[:cols])
        elif full > 1:
            wide = held[: cols * full].reshape(cols, full, LANES)
            parts.extend(wide[:, f, :] for f in range(full))
        if packing.rest:
            spread = jnp.zeros((cols, LANES), F32)
            for j in range(packing.rest_rows):
                line = held[cols * full + j : cols * full + j + 1]
                spread = jnp.where(own & (shared == j), line, spread)
            parts.append(spread)
        return jnp.concatenate(parts, axis=1)

    def body(first, held, step, total):
        i = first + step
        for copy in spec_copies(*held, step, group):
            copy.wait()
        base = i * (group * rows)
        if group * rows % 8 == 0:
            base = pl.multiple_of(base, 8)
        for m in range(sens):
            blocks = [gathered[h * sens + m][pl.ds(base, group * rows), :] for h in range(2)]
            place = slice(m * packing.width, (m + 1) * packing.width)
            for g in range(group):
                x = jnp.concatenate([unpack(block[g * rows : (g + 1) * rows]) for block in blocks], axis=0)
                xh, xl = split(x)
                t = i * group + g
                both = dot_nt(jnp.concatenate([xh, xl], axis=0), oh_ref[t, :, place])
                total = total + (both[: 2 * cols] + both[2 * cols :] + dot_nt(xh, ol_ref[t, :, place]))
        return total

    total = jnp.zeros(out_ref.shape, F32)
    for first, own_chunks, held in sources:
        total = lax.fori_loop(0, own_chunks, functools.partial(body, first, held), total)
    out_ref[...] = total


def whole(array):
    return pl.BlockSpec(array.shape, lambda *_: (0,) * array.ndim)


def swap(size, mask):
    return [(k, k ^ mask) for k in range(size)]


def reduce_near(keep, send, first, size):
    return keep + lax.ppermute(send, "sens", swap(size, first))


def reduce_here(near, second, size):
    per = near.shape[0] // 2
    return near[:per] + lax.ppermute(near[per:], "sens", swap(size, second))


def spread_back(here, first, second, size):
    over = lax.ppermute(here, "sens", swap(size, second))
    back = lax.ppermute(here, "sens", swap(size, first))
    return [here, over, back, lax.ppermute(over, "sens", swap(size, first))]


def shards(records, spec_real, spec_imag, prior_cov, sensor_map, inverse_rows):
    cols, sens_dev, steps = records.shape
    bins, _, par_dev = spec_real.shape
    padded = round_up(bins, 8)
    sens, par = lax.axis_size("sens"), lax.axis_size("par")
    packing = Packing(cols // 2, sens_dev)
    rows_dev, times, sensors = inverse_rows.shape
    quarters = sens == 4 and cols % 8 == 0
    limit = 58 * 2**20

    fwd = forward_table(steps, bins, padded)
    inv = inverse_table(steps, bins, padded)
    fh, fl = (jnp.asarray(part) for part in split_host(fwd))
    ih, il = (jnp.asarray(part) for part in split_host(inv))
    inv_blocks = jnp.asarray(inv.reshape(par, times, 2 * padded).astype(np.float32))

    n_out = 4 if quarters else 1

    by_sensor = jnp.transpose(records, (1, 0, 2))
    by_time = jnp.transpose(inverse_rows, (1, 0, 2))
    block = block_of(bins, 15)
    outside = pl.BlockSpec(memory_space=pltpu.HBM)
    spec_scratch = [
        pltpu.VMEM(spec_real.shape, F32),
        pltpu.VMEM(spec_real.shape, F32),
        pltpu.SemaphoreType.DMA((2, bins // block)),
    ]
    sens_tiles = -(-sens_dev // LANES)
    phase_cost = pl.CostEstimate(
        flops=24 * cols * bins * sens_dev * par_dev, bytes_accessed=8 * bins * sens_dev * par_dev, transcendentals=0
    )
    out_a = [jax.ShapeDtypeStruct((cols // n_out, steps, par_dev), F32)] * n_out
    parts = pl.pallas_call(
        functools.partial(adjoint_kernel, quarters),
        in_specs=[whole(by_sensor), whole(fh), whole(fl), whole(ih), whole(il), outside, outside],
        out_specs=[whole(shape) for shape in out_a],
        out_shape=out_a,
        scratch_shapes=spec_scratch
        + [
            pltpu.VMEM((-(-steps // LANES), sens_dev * cols, LANES), F32),
            pltpu.VMEM((sens_tiles, bins * 2 * cols, LANES), F32),
            pltpu.VMEM((cols * 2 * padded, par_dev), F32),
        ],
        compiler_params=pltpu.CompilerParams(vmem_limit_bytes=limit),
        cost_estimate=phase_cost,
        name="adjoint",
    )(by_sensor, fh, fl, ih, il, spec_real, spec_imag)

    time_block = block_of(times, 4)
    width = sens * packing.width
    moved = jax.ShapeDtypeStruct((times, rows_dev, width), BF16)
    folded = jax.ShapeDtypeStruct((2 * padded, steps), BF16)
    turned = jax.ShapeDtypeStruct((steps, 2 * padded), BF16)
    map_column = sensor_map.reshape(sensors, 1)
    *parts, map_column = lax.optimization_barrier((*parts, map_column))
    chosen = jax.ShapeDtypeStruct((sensors, width), BF16)
    select, th, tl, ih2, il2 = pl.pallas_call(
        functools.partial(tables_kernel, packing),
        in_specs=[whole(map_column), whole(prior_cov), whole(fh), whole(fl), whole(inv_blocks)],
        out_shape=[chosen, folded, folded, turned, turned],
        scratch_shapes=[pltpu.VMEM((steps, 2 * padded), F32)],
        compiler_params=pltpu.CompilerParams(vmem_limit_bytes=limit),
        name="tables",
    )(map_column, prior_cov, fh, fl, inv_blocks)

    blocks = times // time_block
    third = max(blocks // 3, 1)
    cuts = [0, third, 2 * third, blocks] if blocks >= 3 else [0, blocks]

    def move_rows(number, chosen_rows):
        start, stop = cuts[number], cuts[number + 1]
        moved = jax.ShapeDtypeStruct(((stop - start) * time_block, rows_dev, width), BF16)
        return pl.pallas_call(
            rows_kernel,
            grid=(stop - start,),
            in_specs=[
                whole(chosen),
                pl.BlockSpec((time_block, rows_dev, sensors), lambda i: (i + start, 0, 0)),
            ],
            out_specs=[pl.BlockSpec((time_block, rows_dev, width), lambda i: (i, 0, 0))] * 2,
            out_shape=[moved, moved],
            compiler_params=pltpu.CompilerParams(vmem_limit_bytes=limit),
            cost_estimate=pl.CostEstimate(
                flops=4 * rows_dev * moved.shape[0] * sensors * width,
                bytes_accessed=8 * rows_dev * moved.shape[0] * sensors,
                transcendentals=0,
            ),
            name="rows",
        )(chosen_rows, by_time)

    ready = [move_rows(0, select)]
    if quarters and len(cuts) == 4:
        near0 = reduce_near(parts[0], parts[1], 1, sens)
        near1 = reduce_near(parts[2], parts[3], 2, sens)
        near0, near1, th, ready[0], select = lax.optimization_barrier((near0, near1, th, ready[0], select))
        ready.append(move_rows(1, select))
        here0, here1 = reduce_here(near0, 2, sens), reduce_here(near1, 1, sens)
        here0, here1, ready[1], select = lax.optimization_barrier((here0, here1, ready[1], select))
        ready.append(move_rows(2, select))
        pieces = spread_back(here0, 1, 2, sens) + spread_back(here1, 2, 1, sens)
        pieces[-1], ready[2] = lax.optimization_barrier((pieces[-1], ready[2]))
    else:
        pieces = [lax.psum(jnp.concatenate(parts, axis=0), "sens")]
        ready.extend(move_rows(number, select) for number in range(1, len(cuts) - 1))

    shard_rows = times * packing.rows
    half = jax.ShapeDtypeStruct((par // 2 * shard_rows, LANES), F32)
    keep0, keep1, send0, send1 = pl.pallas_call(
        functools.partial(forward_kernel, packing, quarters),
        in_specs=[whole(th), whole(tl), whole(ih2), whole(il2)]
        + [whole(piece) for piece in pieces]
        + [outside, outside],
        out_specs=[whole(half)] * 4,
        out_shape=[half] * 4,
        scratch_shapes=spec_scratch
        + [
            pltpu.VMEM((cols, steps, par_dev), F32),
            pltpu.VMEM((bins * 2 * cols, par_dev), F32),
            pltpu.VMEM((sens_tiles, cols * 2 * padded, LANES), F32),
            pltpu.VMEM((steps, LANES), F32),
        ],
        compiler_params=pltpu.CompilerParams(vmem_limit_bytes=limit),
        cost_estimate=phase_cost,
        name="forward",
    )(th, tl, ih2, il2, *pieces, spec_real, spec_imag)

    def over_pairs(pair, d):
        there = pair[d * shard_rows : (d + 1) * shard_rows]
        return lax.ppermute(there, "par", [(k, (k + 2 * d) % par) for k in range(par)])

    def over_sens(mine):
        return [mine] + [lax.ppermute(mine, "sens", swap(sens, m)) for m in range(1, sens)]

    pair0 = keep0 + lax.ppermute(send0, "par", swap(par, 1))
    pair1 = keep1 + lax.ppermute(send1, "par", swap(par, 1))
    come = [over_pairs(pair0, d) for d in range(1, par // 2)]
    come[0], come[-1], pair1 = lax.optimization_barrier((come[0], come[-1], pair1))
    mine0 = pair0[:shard_rows] + sum(come[1:], come[0])
    mine1 = pair1[:shard_rows] + sum(over_pairs(pair1, d) for d in range(1, par // 2))
    gathered = over_sens(mine0) + over_sens(mine1)

    result = jax.ShapeDtypeStruct((cols, rows_dev), F32)
    partial = pl.pallas_call(
        functools.partial(update_kernel, packing, len(ready)),
        in_specs=[outside] * (2 * len(ready)) + [whole(part) for part in gathered],
        out_shape=result,
        scratch_shapes=[
            pltpu.VMEM(moved.shape, BF16),
            pltpu.VMEM(moved.shape, BF16),
            pltpu.SemaphoreType.DMA((2, blocks)),
        ],
        compiler_params=pltpu.CompilerParams(vmem_limit_bytes=limit),
        cost_estimate=pl.CostEstimate(
            flops=6 * rows_dev * times * cols * width, bytes_accessed=4 * rows_dev * times * width, transcendentals=0
        ),
        name="update",
    )(*(pair[0] for pair in ready), *(pair[1] for pair in ready), *gathered)
    spread = lax.all_to_all(partial.reshape(par, cols // par, rows_dev), "par", 0, 0)
    return jnp.sum(spread, axis=0)


def solution(mesh):
    return jax.shard_map(
        shards,
        mesh=mesh,
        in_specs=(
            P(None, "sens", None),
            P(None, "sens", "par"),
            P(None, "sens", "par"),
            P(),
            P(),
            P("sens", "par", None),
        ),
        out_specs=P("par", "sens"),
        check_vma=False,
    )
```

```python
import functools

import jax
import jax.numpy as jnp
import numpy as np
from jax import lax
from jax.experimental import pallas as pl
from jax.experimental.pallas import tpu as pltpu
from jax.sharding import PartitionSpec as P

F32 = jnp.float32
BF16 = jnp.bfloat16
LANES = 128


def round_up(value, step):
    return (value + step - 1) // step * step


def split(value):
    high = value.astype(BF16)
    low = (value - high.astype(F32)).astype(BF16)
    return high, low


def dot(left, right):
    return lax.dot_general(left, right, (((1,), (0,)), ((), ())), preferred_element_type=F32)


def dot_nt(left, right):
    return lax.dot_general(left, right, (((1,), (1,)), ((), ())), preferred_element_type=F32)


def split_host(table):
    high = table.astype(np.float32).astype(jnp.bfloat16)
    low = (table - high.astype(np.float64)).astype(jnp.bfloat16)
    return high, low


def forward_table(steps, bins, padded):
    length = 2 * steps
    phase = 2.0 * np.pi * ((np.arange(bins)[:, None] * np.arange(steps)[None, :]) % length) / length
    table = np.zeros((2 * padded, steps))
    table[:bins] = np.cos(phase)
    table[padded : padded + bins] = -np.sin(phase)
    return table


def inverse_table(steps, bins, padded):
    length = 2 * steps
    phase = 2.0 * np.pi * ((np.arange(steps)[:, None] * np.arange(bins)[None, :]) % length) / length
    weight = np.full((bins,), 2.0)
    weight[0] = 1.0
    weight[-1] = 1.0
    weight = weight / length
    table = np.zeros((steps, 2 * padded))
    table[:, :bins] = np.cos(phase) * weight
    table[:, padded : padded + bins] = -np.sin(phase) * weight
    return table


def block_of(bins, most):
    return max(size for size in range(1, most + 1) if bins % size == 0)


class Packing:
    def __init__(self, cols, sens_dev):
        self.cols = cols
        self.sens_dev = sens_dev
        self.full = sens_dev // LANES
        self.rest = sens_dev % LANES
        self.share = LANES // self.rest if self.rest else 1
        self.rest_rows = -(-cols // self.share) if self.rest else 0
        self.rows = self.full * cols + self.rest_rows
        self.width = LANES * (self.full + (1 if self.rest else 0))


def lane_tiles(value):
    rows, columns = value.shape
    tiles = []
    for start in range(0, columns, LANES):
        tile = value[:, start : start + LANES]
        short = LANES - tile.shape[1]
        if short:
            tile = jnp.concatenate([tile, jnp.zeros((rows, short), value.dtype)], axis=1)
        tiles.append(tile)
    return tiles


def spec_copies(hbm_refs, vmem_refs, sems, chunk, block):
    part = pl.ds(chunk * block, block)
    return [
        pltpu.make_async_copy(hbm.at[part], vmem.at[part], sems.at[j, chunk])
        for j, (hbm, vmem) in enumerate(zip(hbm_refs, vmem_refs))
    ]


def start_all(hbm_refs, vmem_refs, sems, chunks, block):
    for chunk in range(chunks):
        for copy in spec_copies(hbm_refs, vmem_refs, sems, chunk, block):
            copy.start()


def column_masks(quarters, cols):
    if not quarters:
        return (0, 0)
    index = lax.axis_index("sens")
    bit0, bit1 = index & 1, index >> 1
    unit = cols // 8
    return ((2 * bit0 + bit1) * unit, (2 * bit1 + bit0) * unit)


def adjoint_kernel(quarters, rec_ref, fh_ref, fl_ref, ih_ref, il_ref, sr_hbm, si_hbm, *rest):
    outs, (sr_ref, si_ref, sems, spread, rec_spec, adj) = rest[:-6], rest[-6:]
    sens_dev, cols, steps = rec_ref.shape
    bins, _, par_dev = sr_ref.shape
    chunks = sems.shape[1]
    block = bins // chunks
    padded = adj.shape[0] // cols // 2
    tall = 2 * padded
    half = cols // 2
    masks = column_masks(quarters, cols)
    start_all((sr_hbm, si_hbm), (sr_ref, si_ref), sems, chunks, block)

    every = rec_ref[...].reshape(sens_dev * cols, steps)
    for f, tile in enumerate(lane_tiles(every)):
        spread[f] = tile
    for row in list(range(bins, padded)) + list(range(padded + bins, tall)):
        adj[pl.ds(row, cols, stride=tall), :] = jnp.zeros((cols, par_dev), F32)

    def column(c, _):
        own = [spread[f, pl.ds(c, sens_dev, stride=cols), :] for f in range(spread.shape[0])]
        rh, rl = split(jnp.concatenate(own, axis=1)[:, :steps])
        fh, fl = fh_ref[...], fl_ref[...]
        value = dot_nt(fh, rh) + (dot_nt(fl, rh) + dot_nt(fh, rl))
        for f, tile in enumerate(lane_tiles(value)):
            rec_spec[f, pl.ds(c, bins, stride=2 * cols), :] = tile[:bins]
            rec_spec[f, pl.ds(cols + c, bins, stride=2 * cols), :] = tile[padded : padded + bins]
        return 0

    lax.fori_loop(0, cols, column, 0, unroll=True)

    def chunk_body(chunk, _):
        for copy in spec_copies((sr_hbm, si_hbm), (sr_ref, si_ref), sems, chunk, block):
            copy.wait()
        for i in range(block):
            w = chunk * block + i
            at = pl.ds(pl.multiple_of(w * 2 * cols, 8), 2 * cols)
            x = jnp.concatenate([rec_spec[f, at, :] for f in range(rec_spec.shape[0])], axis=1)[:, :sens_dev]
            xh, xl = split(x)
            sh, sl = split(jnp.concatenate([sr_ref[w], si_ref[w]], axis=1))
            both = dot(jnp.concatenate([xh, xl], axis=0), sh)
            value = both[: 2 * cols] + both[2 * cols :] + dot(xh, sl)
            adj[pl.ds(w, cols, stride=tall), :] = value[:cols, :par_dev] + value[cols:, par_dev:]
            adj[pl.ds(padded + w, cols, stride=tall), :] = value[cols:, :par_dev] - value[:cols, par_dev:]
        return 0

    lax.fori_loop(0, chunks, chunk_body, 0)

    per = cols // len(outs)
    for o, out in enumerate(outs):
        def pair(j, _):
            wide = []
            for e in range(2):
                k = o * per + 2 * j + e
                c = k ^ masks[o * per // half]
                wide.append(adj[pl.ds(pl.multiple_of(c * tall, 8), tall), :])
            ah, al = split(jnp.concatenate(wide, axis=1))
            ih, il = ih_ref[...], il_ref[...]
            value = dot(ih, ah) + (dot(il, ah) + dot(ih, al))
            out[2 * j] = value[:, :par_dev]
            out[2 * j + 1] = value[:, par_dev:]
            return 0

        lax.fori_loop(0, per // 2, pair, 0, unroll=True)


def forward_kernel(packing, quarters, th_ref, tl_ref, ih_ref, il_ref, *rest):
    keep_refs, send_refs = rest[-11:-9], rest[-9:-7]
    (sr_ref, si_ref, sems, whole_ref, field, pred, left) = rest[-7:]
    sr_hbm, si_hbm = rest[-13:-11]
    pieces = rest[:-13]
    cols = 2 * packing.cols
    bins, sens_dev, par_dev = sr_ref.shape
    chunks = sems.shape[1]
    block = bins // chunks
    padded = pred.shape[1] // cols // 2
    tall = 2 * padded
    half = cols // 2
    masks = column_masks(quarters, cols)
    full, width = packing.full, packing.full * LANES
    start_all((sr_hbm, si_hbm), (sr_ref, si_ref), sems, chunks, block)

    per = cols // len(pieces)
    for p, piece in enumerate(pieces):
        for e in range(per):
            k = p * per + e
            whole_ref[k ^ masks[k // half]] = piece[e]
    for row in list(range(bins, padded)) + list(range(padded + bins, tall)):
        for f in range(pred.shape[0]):
            pred[f, pl.ds(row, cols, stride=tall), :] = jnp.zeros((cols, LANES), F32)

    def transform(j, _):
        ah, al = split(jnp.concatenate([whole_ref[2 * j], whole_ref[2 * j + 1]], axis=1))
        th, tl = th_ref[...], tl_ref[...]
        value = dot(th, ah) + (dot(tl, ah) + dot(th, al))
        for e in range(2):
            c = 2 * j + e
            part = value[:, e * par_dev : (e + 1) * par_dev]
            field[pl.ds(c, bins, stride=2 * cols), :] = part[:bins]
            field[pl.ds(cols + c, bins, stride=2 * cols), :] = part[padded : padded + bins]
        return 0

    lax.fori_loop(0, cols // 2, transform, 0, unroll=4)

    def chunk_body(chunk, _):
        for copy in spec_copies((sr_hbm, si_hbm), (sr_ref, si_ref), sems, chunk, block):
            copy.wait()
        for i in range(block):
            w = chunk * block + i
            x = field[pl.ds(pl.multiple_of(w * 2 * cols, 8), 2 * cols), :]
            turned = jnp.concatenate([-x[cols:], x[:cols]], axis=0)
            xh, xl = split(jnp.concatenate([x, turned], axis=1))
            sh, sl = split(jnp.concatenate([sr_ref[w], si_ref[w]], axis=1))
            data = jnp.concatenate(
                [
                    jnp.concatenate([xh, xh], axis=1),
                    jnp.concatenate([xl, jnp.zeros_like(xl)], axis=1),
                ],
                axis=0,
            )
            both = dot_nt(jnp.concatenate([sh, sl], axis=1), data).T
            value = both[: 2 * cols] + both[2 * cols :]
            for f, tile in enumerate(lane_tiles(value)):
                pred[f, pl.ds(w, cols, stride=tall), :] = tile[:cols]
                pred[f, pl.ds(padded + w, cols, stride=tall), :] = tile[cols:]
        return 0

    lax.fori_loop(0, chunks, chunk_body, 0)

    rows = packing.rows
    count = ih_ref.shape[0] // 2
    for column in range(cols):
        keep_ref, send_ref = keep_refs[column // packing.cols], send_refs[column // packing.cols]
        c = column % packing.cols
        wide = [pred[f, column * tall : (column + 1) * tall, :] for f in range(pred.shape[0])]
        ph, pl_low = split(jnp.concatenate(wide, axis=1))
        ih, il = ih_ref[...], il_ref[...]
        value = dot(ih, ph) + (dot(il, ph) + dot(ih, pl_low))
        for f in range(full):
            part = value[:, f * LANES : (f + 1) * LANES]
            keep_ref[pl.ds(c * full + f, count, stride=rows), :] = part[:count]
            send_ref[pl.ds(c * full + f, count, stride=rows), :] = part[count:]
        if packing.rest:
            place = c % packing.share
            part = value[:, width:]
            if place:
                part = pltpu.roll(part, place * packing.rest, 1)
                left[...] += part
            else:
                left[...] = part
            if place == packing.share - 1 or c == packing.cols - 1:
                row = packing.cols * full + c // packing.share
                keep_ref[pl.ds(row, count, stride=rows), :] = left[:count]
                send_ref[pl.ds(row, count, stride=rows), :] = left[count:]


def tables_kernel(packing, map_ref, prior_ref, fh_ref, fl_ref, inv_ref,
                  select, th_ref, tl_ref, ih_ref, il_ref, table):
    blocks = select.shape[1] // packing.width
    times = inv_ref.shape[1]
    lane = lax.broadcasted_iota(jnp.int32, (1, packing.width), 1)
    width = packing.full * LANES
    if packing.rest:
        beyond = lane - width
        folded = width + lax.rem(jnp.maximum(beyond, 0), packing.rest)
        local = jnp.where(beyond >= 0, folded, lane)
        valid = beyond < packing.share * packing.rest
    else:
        local = lane
        valid = lane >= 0
    for m in range(blocks):
        owner = lax.axis_index("sens") ^ m
        wanted = jnp.where(valid, owner * packing.sens_dev + local, -1)
        hit = map_ref[...] == wanted
        select[:, m * packing.width : (m + 1) * packing.width] = jnp.where(hit, 1.0, 0.0).astype(BF16)
    ph, pl_low = split(prior_ref[...])
    folded_table = dot_nt(fh_ref[...], ph) + (dot_nt(fl_ref[...], ph) + dot_nt(fh_ref[...], pl_low))
    th, tl = split(folded_table)
    th_ref[...] = th
    tl_ref[...] = tl
    par = inv_ref.shape[0]
    pairs = par // 2
    place = lax.axis_index("par")
    for r in range(2):
        for d in range(pairs):
            z = lax.rem(place // 2 + d, pairs)
            core = lax.rem(place, 2) ^ r
            j = r * pairs + d
            table[j * times : (j + 1) * times, :] = inv_ref[2 * z + core]
    ih, il = split(table[...])
    ih_ref[...] = ih
    il_ref[...] = il


def rows_kernel(select, rows_ref, oh_ref, ol_ref):
    group, count, sensors = rows_ref.shape
    high, low = split(rows_ref[...].reshape(group * count, sensors))
    moved = dot(jnp.concatenate([high, low], axis=0), select[...]).astype(BF16)
    oh_ref[...] = moved[: group * count].reshape(oh_ref.shape)
    ol_ref[...] = moved[group * count :].reshape(ol_ref.shape)


def update_kernel(packing, count, *rest):
    high, low, gathered = rest[:count], rest[count : 2 * count], rest[2 * count : -4]
    out_ref, oh_ref, ol_ref, sems = rest[-4:]
    times = oh_ref.shape[0]
    chunks = sems.shape[1]
    group = times // chunks
    sources, first = [], 0
    for hbm in zip(high, low):
        part = pl.ds(first * group, hbm[0].shape[0])
        own_chunks = hbm[0].shape[0] // group
        held = (hbm, (oh_ref.at[part], ol_ref.at[part]), sems.at[:, pl.ds(first, own_chunks)])
        start_all(*held, own_chunks, group)
        sources.append((first, own_chunks, held))
        first += own_chunks
    cols, rows, full = packing.cols, packing.rows, packing.full
    sens = len(gathered) // 2
    if packing.rest:
        row = lax.broadcasted_iota(jnp.int32, (cols, LANES), 0)
        lane = lax.broadcasted_iota(jnp.int32, (cols, LANES), 1)
        own = lax.rem(row, packing.share) == lane // packing.rest
        shared = row // packing.share

    def unpack(held):
        parts = []
        if full == 1:
            parts.append(held[:cols])
        elif full > 1:
            wide = held[: cols * full].reshape(cols, full, LANES)
            parts.extend(wide[:, f, :] for f in range(full))
        if packing.rest:
            spread = jnp.zeros((cols, LANES), F32)
            for j in range(packing.rest_rows):
                line = held[cols * full + j : cols * full + j + 1]
                spread = jnp.where(own & (shared == j), line, spread)
            parts.append(spread)
        return jnp.concatenate(parts, axis=1)

    def body(first, held, step, total):
        i = first + step
        for copy in spec_copies(*held, step, group):
            copy.wait()
        base = i * (group * rows)
        if group * rows % 8 == 0:
            base = pl.multiple_of(base, 8)
        for m in range(sens):
            blocks = [gathered[h * sens + m][pl.ds(base, group * rows), :] for h in range(2)]
            place = slice(m * packing.width, (m + 1) * packing.width)
            for g in range(group):
                x = jnp.concatenate([unpack(block[g * rows : (g + 1) * rows]) for block in blocks], axis=0)
                xh, xl = split(x)
                t = i * group + g
                both = dot_nt(jnp.concatenate([xh, xl], axis=0), oh_ref[t, :, place])
                total = total + (both[: 2 * cols] + both[2 * cols :] + dot_nt(xh, ol_ref[t, :, place]))
        return total

    total = jnp.zeros(out_ref.shape, F32)
    for first, own_chunks, held in sources:
        total = lax.fori_loop(0, own_chunks, functools.partial(body, first, held), total)
    out_ref[...] = total


def whole(array):
    return pl.BlockSpec(array.shape, lambda *_: (0,) * array.ndim)


def swap(size, mask):
    return [(k, k ^ mask) for k in range(size)]


def reduce_near(keep, send, first, size):
    return keep + lax.ppermute(send, "sens", swap(size, first))


def reduce_here(near, second, size):
    per = near.shape[0] // 2
    return near[:per] + lax.ppermute(near[per:], "sens", swap(size, second))


def spread_back(here, first, second, size):
    over = lax.ppermute(here, "sens", swap(size, second))
    back = lax.ppermute(here, "sens", swap(size, first))
    return [here, over, back, lax.ppermute(over, "sens", swap(size, first))]


def shards(records, spec_real, spec_imag, prior_cov, sensor_map, inverse_rows):
    cols, sens_dev, steps = records.shape
    bins, _, par_dev = spec_real.shape
    padded = round_up(bins, 8)
    sens, par = lax.axis_size("sens"), lax.axis_size("par")
    packing = Packing(cols // 2, sens_dev)
    rows_dev, times, sensors = inverse_rows.shape
    quarters = sens == 4 and cols % 8 == 0
    limit = 58 * 2**20

    fwd = forward_table(steps, bins, padded)
    inv = inverse_table(steps, bins, padded)
    fh, fl = (jnp.asarray(part) for part in split_host(fwd))
    ih, il = (jnp.asarray(part) for part in split_host(inv))
    inv_blocks = jnp.asarray(inv.reshape(par, times, 2 * padded).astype(np.float32))

    n_out = 4 if quarters else 1

    by_sensor = jnp.transpose(records, (1, 0, 2))
    by_time = jnp.transpose(inverse_rows, (1, 0, 2))
    block = block_of(bins, 15)
    outside = pl.BlockSpec(memory_space=pltpu.HBM)
    spec_scratch = [
        pltpu.VMEM(spec_real.shape, F32),
        pltpu.VMEM(spec_real.shape, F32),
        pltpu.SemaphoreType.DMA((2, bins // block)),
    ]
    sens_tiles = -(-sens_dev // LANES)
    phase_cost = pl.CostEstimate(
        flops=24 * cols * bins * sens_dev * par_dev, bytes_accessed=8 * bins * sens_dev * par_dev, transcendentals=0
    )
    out_a = [jax.ShapeDtypeStruct((cols // n_out, steps, par_dev), F32)] * n_out
    parts = pl.pallas_call(
        functools.partial(adjoint_kernel, quarters),
        in_specs=[whole(by_sensor), whole(fh), whole(fl), whole(ih), whole(il), outside, outside],
        out_specs=[whole(shape) for shape in out_a],
        out_shape=out_a,
        scratch_shapes=spec_scratch
        + [
            pltpu.VMEM((-(-steps // LANES), sens_dev * cols, LANES), F32),
            pltpu.VMEM((sens_tiles, bins * 2 * cols, LANES), F32),
            pltpu.VMEM((cols * 2 * padded, par_dev), F32),
        ],
        compiler_params=pltpu.CompilerParams(vmem_limit_bytes=limit),
        cost_estimate=phase_cost,
        name="adjoint",
    )(by_sensor, fh, fl, ih, il, spec_real, spec_imag)

    time_block = block_of(times, 4)
    width = sens * packing.width
    moved = jax.ShapeDtypeStruct((times, rows_dev, width), BF16)
    folded = jax.ShapeDtypeStruct((2 * padded, steps), BF16)
    turned = jax.ShapeDtypeStruct((steps, 2 * padded), BF16)
    map_column = sensor_map.reshape(sensors, 1)
    *parts, map_column = lax.optimization_barrier((*parts, map_column))
    chosen = jax.ShapeDtypeStruct((sensors, width), BF16)
    select, th, tl, ih2, il2 = pl.pallas_call(
        functools.partial(tables_kernel, packing),
        in_specs=[whole(map_column), whole(prior_cov), whole(fh), whole(fl), whole(inv_blocks)],
        out_shape=[chosen, folded, folded, turned, turned],
        scratch_shapes=[pltpu.VMEM((steps, 2 * padded), F32)],
        compiler_params=pltpu.CompilerParams(vmem_limit_bytes=limit),
        name="tables",
    )(map_column, prior_cov, fh, fl, inv_blocks)

    blocks = times // time_block
    third = max(blocks // 3, 1)
    cuts = [0, third, 2 * third, blocks] if blocks >= 3 else [0, blocks]

    def move_rows(number, chosen_rows):
        start, stop = cuts[number], cuts[number + 1]
        moved = jax.ShapeDtypeStruct(((stop - start) * time_block, rows_dev, width), BF16)
        return pl.pallas_call(
            rows_kernel,
            grid=(stop - start,),
            in_specs=[
                whole(chosen),
                pl.BlockSpec((time_block, rows_dev, sensors), lambda i: (i + start, 0, 0)),
            ],
            out_specs=[pl.BlockSpec((time_block, rows_dev, width), lambda i: (i, 0, 0))] * 2,
            out_shape=[moved, moved],
            compiler_params=pltpu.CompilerParams(vmem_limit_bytes=limit),
            cost_estimate=pl.CostEstimate(
                flops=4 * rows_dev * moved.shape[0] * sensors * width,
                bytes_accessed=8 * rows_dev * moved.shape[0] * sensors,
                transcendentals=0,
            ),
            name="rows",
        )(chosen_rows, by_time)

    ready = [move_rows(0, select)]
    if quarters and len(cuts) == 4:
        near0 = reduce_near(parts[0], parts[1], 1, sens)
        near1 = reduce_near(parts[2], parts[3], 2, sens)
        near0, near1, th, ready[0], select = lax.optimization_barrier((near0, near1, th, ready[0], select))
        ready.append(move_rows(1, select))
        here0, here1 = reduce_here(near0, 2, sens), reduce_here(near1, 1, sens)
        here0, here1, ready[1], select = lax.optimization_barrier((here0, here1, ready[1], select))
        ready.append(move_rows(2, select))
        pieces = spread_back(here0, 1, 2, sens) + spread_back(here1, 2, 1, sens)
        pieces[-1], ready[2] = lax.optimization_barrier((pieces[-1], ready[2]))
    else:
        pieces = [lax.psum(jnp.concatenate(parts, axis=0), "sens")]
        ready.extend(move_rows(number, select) for number in range(1, len(cuts) - 1))

    shard_rows = times * packing.rows
    half = jax.ShapeDtypeStruct((par // 2 * shard_rows, LANES), F32)
    keep0, keep1, send0, send1 = pl.pallas_call(
        functools.partial(forward_kernel, packing, quarters),
        in_specs=[whole(th), whole(tl), whole(ih2), whole(il2)]
        + [whole(piece) for piece in pieces]
        + [outside, outside],
        out_specs=[whole(half)] * 4,
        out_shape=[half] * 4,
        scratch_shapes=spec_scratch
        + [
            pltpu.VMEM((cols, steps, par_dev), F32),
            pltpu.VMEM((bins * 2 * cols, par_dev), F32),
            pltpu.VMEM((sens_tiles, cols * 2 * padded, LANES), F32),
            pltpu.VMEM((steps, LANES), F32),
        ],
        compiler_params=pltpu.CompilerParams(vmem_limit_bytes=limit),
        cost_estimate=phase_cost,
        name="forward",
    )(th, tl, ih2, il2, *pieces, spec_real, spec_imag)

    def over_pairs(pair, d):
        there = pair[d * shard_rows : (d + 1) * shard_rows]
        return lax.ppermute(there, "par", [(k, (k + 2 * d) % par) for k in range(par)])

    def over_sens(mine):
        return [mine] + [lax.ppermute(mine, "sens", swap(sens, m)) for m in range(1, sens)]

    pair0 = keep0 + lax.ppermute(send0, "par", swap(par, 1))
    pair1 = keep1 + lax.ppermute(send1, "par", swap(par, 1))
    come = [over_pairs(pair0, d) for d in range(1, par // 2)]
    mine0 = pair0[:shard_rows] + sum(come[1:], come[0])
    mine1 = pair1[:shard_rows] + sum(over_pairs(pair1, d) for d in range(1, par // 2))
    gathered = over_sens(mine0) + over_sens(mine1)

    result = jax.ShapeDtypeStruct((cols, rows_dev), F32)
    partial = pl.pallas_call(
        functools.partial(update_kernel, packing, len(ready)),
        in_specs=[outside] * (2 * len(ready)) + [whole(part) for part in gathered],
        out_shape=result,
        scratch_shapes=[
            pltpu.VMEM(moved.shape, BF16),
            pltpu.VMEM(moved.shape, BF16),
            pltpu.SemaphoreType.DMA((2, blocks)),
        ],
        compiler_params=pltpu.CompilerParams(vmem_limit_bytes=limit),
        cost_estimate=pl.CostEstimate(
            flops=6 * rows_dev * times * cols * width, bytes_accessed=4 * rows_dev * times * width, transcendentals=0
        ),
        name="update",
    )(*(pair[0] for pair in ready), *(pair[1] for pair in ready), *gathered)
    spread = lax.all_to_all(partial.reshape(par, cols // par, rows_dev), "par", 0, 0)
    return jnp.sum(spread, axis=0)


def solution(mesh):
    return jax.shard_map(
        shards,
        mesh=mesh,
        in_specs=(
            P(None, "sens", None),
            P(None, "sens", "par"),
            P(None, "sens", "par"),
            P(),
            P(),
            P("sens", "par", None),
        ),
        out_specs=P("par", "sens"),
        check_vma=False,
    )
```

```python
import functools

import jax
import jax.numpy as jnp
import numpy as np
from jax import lax
from jax.experimental import pallas as pl
from jax.experimental.pallas import tpu as pltpu
from jax.sharding import PartitionSpec as P

F32 = jnp.float32
BF16 = jnp.bfloat16
LANES = 128


def round_up(value, step):
    return (value + step - 1) // step * step


def split(value):
    high = value.astype(BF16)
    low = (value - high.astype(F32)).astype(BF16)
    return high, low


def dot(left, right):
    return lax.dot_general(left, right, (((1,), (0,)), ((), ())), preferred_element_type=F32)


def dot_nt(left, right):
    return lax.dot_general(left, right, (((1,), (1,)), ((), ())), preferred_element_type=F32)


def split_host(table):
    high = table.astype(np.float32).astype(jnp.bfloat16)
    low = (table - high.astype(np.float64)).astype(jnp.bfloat16)
    return high, low


def forward_table(steps, bins, padded):
    length = 2 * steps
    phase = 2.0 * np.pi * ((np.arange(bins)[:, None] * np.arange(steps)[None, :]) % length) / length
    table = np.zeros((2 * padded, steps))
    table[:bins] = np.cos(phase)
    table[padded : padded + bins] = -np.sin(phase)
    return table


def inverse_table(steps, bins, padded):
    length = 2 * steps
    phase = 2.0 * np.pi * ((np.arange(steps)[:, None] * np.arange(bins)[None, :]) % length) / length
    weight = np.full((bins,), 2.0)
    weight[0] = 1.0
    weight[-1] = 1.0
    weight = weight / length
    table = np.zeros((steps, 2 * padded))
    table[:, :bins] = np.cos(phase) * weight
    table[:, padded : padded + bins] = -np.sin(phase) * weight
    return table


def block_of(bins, most):
    return max(size for size in range(1, most + 1) if bins % size == 0)


class Packing:
    def __init__(self, cols, sens_dev):
        self.cols = cols
        self.sens_dev = sens_dev
        self.full = sens_dev // LANES
        self.rest = sens_dev % LANES
        self.share = LANES // self.rest if self.rest else 1
        self.rest_rows = -(-cols // self.share) if self.rest else 0
        self.rows = self.full * cols + self.rest_rows
        self.width = LANES * (self.full + (1 if self.rest else 0))


def lane_tiles(value):
    rows, columns = value.shape
    tiles = []
    for start in range(0, columns, LANES):
        tile = value[:, start : start + LANES]
        short = LANES - tile.shape[1]
        if short:
            tile = jnp.concatenate([tile, jnp.zeros((rows, short), value.dtype)], axis=1)
        tiles.append(tile)
    return tiles


def spec_copies(hbm_refs, vmem_refs, sems, chunk, block):
    part = pl.ds(chunk * block, block)
    return [
        pltpu.make_async_copy(hbm.at[part], vmem.at[part], sems.at[j, chunk])
        for j, (hbm, vmem) in enumerate(zip(hbm_refs, vmem_refs))
    ]


def start_all(hbm_refs, vmem_refs, sems, chunks, block):
    for chunk in range(chunks):
        for copy in spec_copies(hbm_refs, vmem_refs, sems, chunk, block):
            copy.start()


def column_masks(quarters, cols):
    if not quarters:
        return (0, 0)
    index = lax.axis_index("sens")
    bit0, bit1 = index & 1, index >> 1
    unit = cols // 8
    return ((2 * bit0 + bit1) * unit, (2 * bit1 + bit0) * unit)


def adjoint_kernel(quarters, rec_ref, fh_ref, fl_ref, ih_ref, il_ref, sr_hbm, si_hbm, *rest):
    outs, (sr_ref, si_ref, sems, spread, rec_spec, adj) = rest[:-6], rest[-6:]
    sens_dev, cols, steps = rec_ref.shape
    bins, _, par_dev = sr_ref.shape
    chunks = sems.shape[1]
    block = bins // chunks
    padded = adj.shape[0] // cols // 2
    tall = 2 * padded
    half = cols // 2
    masks = column_masks(quarters, cols)
    start_all((sr_hbm, si_hbm), (sr_ref, si_ref), sems, chunks, block)

    every = rec_ref[...].reshape(sens_dev * cols, steps)
    for f, tile in enumerate(lane_tiles(every)):
        spread[f] = tile
    for row in list(range(bins, padded)) + list(range(padded + bins, tall)):
        adj[pl.ds(row, cols, stride=tall), :] = jnp.zeros((cols, par_dev), F32)

    def column(c, _):
        own = [spread[f, pl.ds(c, sens_dev, stride=cols), :] for f in range(spread.shape[0])]
        rh, rl = split(jnp.concatenate(own, axis=1)[:, :steps])
        fh, fl = fh_ref[...], fl_ref[...]
        value = dot_nt(fh, rh) + (dot_nt(fl, rh) + dot_nt(fh, rl))
        for f, tile in enumerate(lane_tiles(value)):
            rec_spec[f, pl.ds(c, bins, stride=2 * cols), :] = tile[:bins]
            rec_spec[f, pl.ds(cols + c, bins, stride=2 * cols), :] = tile[padded : padded + bins]
        return 0

    lax.fori_loop(0, cols, column, 0, unroll=True)

    def chunk_body(chunk, _):
        for copy in spec_copies((sr_hbm, si_hbm), (sr_ref, si_ref), sems, chunk, block):
            copy.wait()
        for i in range(block):
            w = chunk * block + i
            at = pl.ds(pl.multiple_of(w * 2 * cols, 8), 2 * cols)
            x = jnp.concatenate([rec_spec[f, at, :] for f in range(rec_spec.shape[0])], axis=1)[:, :sens_dev]
            xh, xl = split(x)
            sh, sl = split(jnp.concatenate([sr_ref[w], si_ref[w]], axis=1))
            both = dot(jnp.concatenate([xh, xl], axis=0), sh)
            value = both[: 2 * cols] + both[2 * cols :] + dot(xh, sl)
            adj[pl.ds(w, cols, stride=tall), :] = value[:cols, :par_dev] + value[cols:, par_dev:]
            adj[pl.ds(padded + w, cols, stride=tall), :] = value[cols:, :par_dev] - value[:cols, par_dev:]
        return 0

    lax.fori_loop(0, chunks, chunk_body, 0)

    per = cols // len(outs)
    for o, out in enumerate(outs):
        def pair(j, _):
            wide = []
            for e in range(2):
                k = o * per + 2 * j + e
                c = k ^ masks[o * per // half]
                wide.append(adj[pl.ds(pl.multiple_of(c * tall, 8), tall), :])
            ah, al = split(jnp.concatenate(wide, axis=1))
            ih, il = ih_ref[...], il_ref[...]
            value = dot(ih, ah) + (dot(il, ah) + dot(ih, al))
            out[2 * j] = value[:, :par_dev]
            out[2 * j + 1] = value[:, par_dev:]
            return 0

        lax.fori_loop(0, per // 2, pair, 0, unroll=True)


def forward_kernel(packing, quarters, th_ref, tl_ref, ih_ref, il_ref, *rest):
    keep_refs, send_refs = rest[-11:-9], rest[-9:-7]
    (sr_ref, si_ref, sems, whole_ref, field, pred, left) = rest[-7:]
    sr_hbm, si_hbm = rest[-13:-11]
    pieces = rest[:-13]
    cols = 2 * packing.cols
    bins, sens_dev, par_dev = sr_ref.shape
    chunks = sems.shape[1]
    block = bins // chunks
    padded = pred.shape[1] // cols // 2
    tall = 2 * padded
    half = cols // 2
    masks = column_masks(quarters, cols)
    full, width = packing.full, packing.full * LANES
    start_all((sr_hbm, si_hbm), (sr_ref, si_ref), sems, chunks, block)

    per = cols // len(pieces)
    for p, piece in enumerate(pieces):
        for e in range(per):
            k = p * per + e
            whole_ref[k ^ masks[k // half]] = piece[e]
    for row in list(range(bins, padded)) + list(range(padded + bins, tall)):
        for f in range(pred.shape[0]):
            pred[f, pl.ds(row, cols, stride=tall), :] = jnp.zeros((cols, LANES), F32)

    def transform(j, _):
        ah, al = split(jnp.concatenate([whole_ref[2 * j], whole_ref[2 * j + 1]], axis=1))
        th, tl = th_ref[...], tl_ref[...]
        value = dot(th, ah) + (dot(tl, ah) + dot(th, al))
        for e in range(2):
            c = 2 * j + e
            part = value[:, e * par_dev : (e + 1) * par_dev]
            field[pl.ds(c, bins, stride=2 * cols), :] = part[:bins]
            field[pl.ds(cols + c, bins, stride=2 * cols), :] = part[padded : padded + bins]
        return 0

    lax.fori_loop(0, cols // 2, transform, 0, unroll=4)

    def chunk_body(chunk, _):
        for copy in spec_copies((sr_hbm, si_hbm), (sr_ref, si_ref), sems, chunk, block):
            copy.wait()
        for i in range(block):
            w = chunk * block + i
            x = field[pl.ds(pl.multiple_of(w * 2 * cols, 8), 2 * cols), :]
            turned = jnp.concatenate([-x[cols:], x[:cols]], axis=0)
            xh, xl = split(jnp.concatenate([x, turned], axis=1))
            sh, sl = split(jnp.concatenate([sr_ref[w], si_ref[w]], axis=1))
            data = jnp.concatenate(
                [
                    jnp.concatenate([xh, xh], axis=1),
                    jnp.concatenate([xl, jnp.zeros_like(xl)], axis=1),
                ],
                axis=0,
            )
            both = dot_nt(jnp.concatenate([sh, sl], axis=1), data).T
            value = both[: 2 * cols] + both[2 * cols :]
            for f, tile in enumerate(lane_tiles(value)):
                pred[f, pl.ds(w, cols, stride=tall), :] = tile[:cols]
                pred[f, pl.ds(padded + w, cols, stride=tall), :] = tile[cols:]
        return 0

    lax.fori_loop(0, chunks, chunk_body, 0)

    rows = packing.rows
    count = ih_ref.shape[0] // 2
    for column in range(cols):
        keep_ref, send_ref = keep_refs[column // packing.cols], send_refs[column // packing.cols]
        c = column % packing.cols
        wide = [pred[f, column * tall : (column + 1) * tall, :] for f in range(pred.shape[0])]
        ph, pl_low = split(jnp.concatenate(wide, axis=1))
        ih, il = ih_ref[...], il_ref[...]
        value = dot(ih, ph) + (dot(il, ph) + dot(ih, pl_low))
        for f in range(full):
            part = value[:, f * LANES : (f + 1) * LANES]
            keep_ref[pl.ds(c * full + f, count, stride=rows), :] = part[:count]
            send_ref[pl.ds(c * full + f, count, stride=rows), :] = part[count:]
        if packing.rest:
            place = c % packing.share
            part = value[:, width:]
            if place:
                part = pltpu.roll(part, place * packing.rest, 1)
                left[...] += part
            else:
                left[...] = part
            if place == packing.share - 1 or c == packing.cols - 1:
                row = packing.cols * full + c // packing.share
                keep_ref[pl.ds(row, count, stride=rows), :] = left[:count]
                send_ref[pl.ds(row, count, stride=rows), :] = left[count:]


def tables_kernel(packing, map_ref, prior_ref, fh_ref, fl_ref, inv_ref,
                  select, th_ref, tl_ref, ih_ref, il_ref, table):
    blocks = select.shape[1] // packing.width
    times = inv_ref.shape[1]
    lane = lax.broadcasted_iota(jnp.int32, (1, packing.width), 1)
    width = packing.full * LANES
    if packing.rest:
        beyond = lane - width
        folded = width + lax.rem(jnp.maximum(beyond, 0), packing.rest)
        local = jnp.where(beyond >= 0, folded, lane)
        valid = beyond < packing.share * packing.rest
    else:
        local = lane
        valid = lane >= 0
    for m in range(blocks):
        owner = lax.axis_index("sens") ^ m
        wanted = jnp.where(valid, owner * packing.sens_dev + local, -1)
        hit = map_ref[...] == wanted
        select[:, m * packing.width : (m + 1) * packing.width] = jnp.where(hit, 1.0, 0.0).astype(BF16)
    ph, pl_low = split(prior_ref[...])
    folded_table = dot_nt(fh_ref[...], ph) + (dot_nt(fl_ref[...], ph) + dot_nt(fh_ref[...], pl_low))
    th, tl = split(folded_table)
    th_ref[...] = th
    tl_ref[...] = tl
    par = inv_ref.shape[0]
    pairs = par // 2
    place = lax.axis_index("par")
    for r in range(2):
        for d in range(pairs):
            z = lax.rem(place // 2 + d, pairs)
            core = lax.rem(place, 2) ^ r
            j = r * pairs + d
            table[j * times : (j + 1) * times, :] = inv_ref[2 * z + core]
    ih, il = split(table[...])
    ih_ref[...] = ih
    il_ref[...] = il


def rows_kernel(select, rows_ref, oh_ref, ol_ref):
    group, count, sensors = rows_ref.shape
    high, low = split(rows_ref[...].reshape(group * count, sensors))
    moved = dot(jnp.concatenate([high, low], axis=0), select[...]).astype(BF16)
    oh_ref[...] = moved[: group * count].reshape(oh_ref.shape)
    ol_ref[...] = moved[group * count :].reshape(ol_ref.shape)


def update_kernel(packing, count, *rest):
    high, low, gathered = rest[:count], rest[count : 2 * count], rest[2 * count : -4]
    out_ref, oh_ref, ol_ref, sems = rest[-4:]
    times = oh_ref.shape[0]
    chunks = sems.shape[1]
    group = times // chunks
    sources, first = [], 0
    for hbm in zip(high, low):
        part = pl.ds(first * group, hbm[0].shape[0])
        own_chunks = hbm[0].shape[0] // group
        held = (hbm, (oh_ref.at[part], ol_ref.at[part]), sems.at[:, pl.ds(first, own_chunks)])
        start_all(*held, own_chunks, group)
        sources.append((first, own_chunks, held))
        first += own_chunks
    cols, rows, full = packing.cols, packing.rows, packing.full
    sens = len(gathered) // 2
    if packing.rest:
        row = lax.broadcasted_iota(jnp.int32, (cols, LANES), 0)
        lane = lax.broadcasted_iota(jnp.int32, (cols, LANES), 1)
        own = lax.rem(row, packing.share) == lane // packing.rest
        shared = row // packing.share

    def unpack(held):
        parts = []
        if full == 1:
            parts.append(held[:cols])
        elif full > 1:
            wide = held[: cols * full].reshape(cols, full, LANES)
            parts.extend(wide[:, f, :] for f in range(full))
        if packing.rest:
            spread = jnp.zeros((cols, LANES), F32)
            for j in range(packing.rest_rows):
                line = held[cols * full + j : cols * full + j + 1]
                spread = jnp.where(own & (shared == j), line, spread)
            parts.append(spread)
        return jnp.concatenate(parts, axis=1)

    def body(first, held, step, total):
        i = first + step
        for copy in spec_copies(*held, step, group):
            copy.wait()
        base = i * (group * rows)
        if group * rows % 8 == 0:
            base = pl.multiple_of(base, 8)
        for m in range(sens):
            blocks = [gathered[h * sens + m][pl.ds(base, group * rows), :] for h in range(2)]
            place = slice(m * packing.width, (m + 1) * packing.width)
            for g in range(group):
                x = jnp.concatenate([unpack(block[g * rows : (g + 1) * rows]) for block in blocks], axis=0)
                xh, xl = split(x)
                t = i * group + g
                both = dot_nt(jnp.concatenate([xh, xl], axis=0), oh_ref[t, :, place])
                total = total + (both[: 2 * cols] + both[2 * cols :] + dot_nt(xh, ol_ref[t, :, place]))
        return total

    total = jnp.zeros(out_ref.shape, F32)
    for first, own_chunks, held in sources:
        total = lax.fori_loop(0, own_chunks, functools.partial(body, first, held), total)
    out_ref[...] = total


def whole(array):
    return pl.BlockSpec(array.shape, lambda *_: (0,) * array.ndim)


def swap(size, mask):
    return [(k, k ^ mask) for k in range(size)]


def reduce_near(keep, send, first, size):
    return keep + lax.ppermute(send, "sens", swap(size, first))


def reduce_here(near, second, size):
    per = near.shape[0] // 2
    return near[:per] + lax.ppermute(near[per:], "sens", swap(size, second))


def spread_back(here, first, second, size):
    over = lax.ppermute(here, "sens", swap(size, second))
    back = lax.ppermute(here, "sens", swap(size, first))
    return [here, over, back, lax.ppermute(over, "sens", swap(size, first))]


def shards(records, spec_real, spec_imag, prior_cov, sensor_map, inverse_rows):
    cols, sens_dev, steps = records.shape
    bins, _, par_dev = spec_real.shape
    padded = round_up(bins, 8)
    sens, par = lax.axis_size("sens"), lax.axis_size("par")
    packing = Packing(cols // 2, sens_dev)
    rows_dev, times, sensors = inverse_rows.shape
    quarters = sens == 4 and cols % 8 == 0
    limit = 58 * 2**20

    fwd = forward_table(steps, bins, padded)
    inv = inverse_table(steps, bins, padded)
    fh, fl = (jnp.asarray(part) for part in split_host(fwd))
    ih, il = (jnp.asarray(part) for part in split_host(inv))
    inv_blocks = jnp.asarray(inv.reshape(par, times, 2 * padded).astype(np.float32))

    n_out = 4 if quarters else 1

    by_sensor = jnp.transpose(records, (1, 0, 2))
    by_time = jnp.transpose(inverse_rows, (1, 0, 2))
    block = block_of(bins, 25)
    outside = pl.BlockSpec(memory_space=pltpu.HBM)
    spec_scratch = [
        pltpu.VMEM(spec_real.shape, F32),
        pltpu.VMEM(spec_real.shape, F32),
        pltpu.SemaphoreType.DMA((2, bins // block)),
    ]
    sens_tiles = -(-sens_dev // LANES)
    phase_cost = pl.CostEstimate(
        flops=24 * cols * bins * sens_dev * par_dev, bytes_accessed=8 * bins * sens_dev * par_dev, transcendentals=0
    )
    out_a = [jax.ShapeDtypeStruct((cols // n_out, steps, par_dev), F32)] * n_out
    parts = pl.pallas_call(
        functools.partial(adjoint_kernel, quarters),
        in_specs=[whole(by_sensor), whole(fh), whole(fl), whole(ih), whole(il), outside, outside],
        out_specs=[whole(shape) for shape in out_a],
        out_shape=out_a,
        scratch_shapes=spec_scratch
        + [
            pltpu.VMEM((-(-steps // LANES), sens_dev * cols, LANES), F32),
            pltpu.VMEM((sens_tiles, bins * 2 * cols, LANES), F32),
            pltpu.VMEM((cols * 2 * padded, par_dev), F32),
        ],
        compiler_params=pltpu.CompilerParams(vmem_limit_bytes=limit),
        cost_estimate=phase_cost,
        name="adjoint",
    )(by_sensor, fh, fl, ih, il, spec_real, spec_imag)

    time_block = block_of(times, 4)
    width = sens * packing.width
    moved = jax.ShapeDtypeStruct((times, rows_dev, width), BF16)
    folded = jax.ShapeDtypeStruct((2 * padded, steps), BF16)
    turned = jax.ShapeDtypeStruct((steps, 2 * padded), BF16)
    map_column = sensor_map.reshape(sensors, 1)
    *parts, map_column = lax.optimization_barrier((*parts, map_column))
    chosen = jax.ShapeDtypeStruct((sensors, width), BF16)
    select, th, tl, ih2, il2 = pl.pallas_call(
        functools.partial(tables_kernel, packing),
        in_specs=[whole(map_column), whole(prior_cov), whole(fh), whole(fl), whole(inv_blocks)],
        out_shape=[chosen, folded, folded, turned, turned],
        scratch_shapes=[pltpu.VMEM((steps, 2 * padded), F32)],
        compiler_params=pltpu.CompilerParams(vmem_limit_bytes=limit),
        name="tables",
    )(map_column, prior_cov, fh, fl, inv_blocks)

    blocks = times // time_block
    third = max(blocks // 3, 1)
    cuts = [0, third, 2 * third, blocks] if blocks >= 3 else [0, blocks]

    def move_rows(number, chosen_rows):
        start, stop = cuts[number], cuts[number + 1]
        moved = jax.ShapeDtypeStruct(((stop - start) * time_block, rows_dev, width), BF16)
        return pl.pallas_call(
            rows_kernel,
            grid=(stop - start,),
            in_specs=[
                whole(chosen),
                pl.BlockSpec((time_block, rows_dev, sensors), lambda i: (i + start, 0, 0)),
            ],
            out_specs=[pl.BlockSpec((time_block, rows_dev, width), lambda i: (i, 0, 0))] * 2,
            out_shape=[moved, moved],
            compiler_params=pltpu.CompilerParams(vmem_limit_bytes=limit),
            cost_estimate=pl.CostEstimate(
                flops=4 * rows_dev * moved.shape[0] * sensors * width,
                bytes_accessed=8 * rows_dev * moved.shape[0] * sensors,
                transcendentals=0,
            ),
            name="rows",
        )(chosen_rows, by_time)

    ready = [move_rows(0, select)]
    if quarters and len(cuts) == 4:
        near0 = reduce_near(parts[0], parts[1], 1, sens)
        near1 = reduce_near(parts[2], parts[3], 2, sens)
        near0, near1, th, ready[0], select = lax.optimization_barrier((near0, near1, th, ready[0], select))
        ready.append(move_rows(1, select))
        here0, here1 = reduce_here(near0, 2, sens), reduce_here(near1, 1, sens)
        here0, here1, ready[1], select = lax.optimization_barrier((here0, here1, ready[1], select))
        ready.append(move_rows(2, select))
        pieces = spread_back(here0, 1, 2, sens) + spread_back(here1, 2, 1, sens)
        pieces[-1], ready[2] = lax.optimization_barrier((pieces[-1], ready[2]))
    else:
        pieces = [lax.psum(jnp.concatenate(parts, axis=0), "sens")]
        ready.extend(move_rows(number, select) for number in range(1, len(cuts) - 1))

    shard_rows = times * packing.rows
    half = jax.ShapeDtypeStruct((par // 2 * shard_rows, LANES), F32)
    keep0, keep1, send0, send1 = pl.pallas_call(
        functools.partial(forward_kernel, packing, quarters),
        in_specs=[whole(th), whole(tl), whole(ih2), whole(il2)]
        + [whole(piece) for piece in pieces]
        + [outside, outside],
        out_specs=[whole(half)] * 4,
        out_shape=[half] * 4,
        scratch_shapes=spec_scratch
        + [
            pltpu.VMEM((cols, steps, par_dev), F32),
            pltpu.VMEM((bins * 2 * cols, par_dev), F32),
            pltpu.VMEM((sens_tiles, cols * 2 * padded, LANES), F32),
            pltpu.VMEM((steps, LANES), F32),
        ],
        compiler_params=pltpu.CompilerParams(vmem_limit_bytes=limit),
        cost_estimate=phase_cost,
        name="forward",
    )(th, tl, ih2, il2, *pieces, spec_real, spec_imag)

    def over_pairs(pair, d):
        there = pair[d * shard_rows : (d + 1) * shard_rows]
        return lax.ppermute(there, "par", [(k, (k + 2 * d) % par) for k in range(par)])

    def over_sens(mine):
        return [mine] + [lax.ppermute(mine, "sens", swap(sens, m)) for m in range(1, sens)]

    pair0 = keep0 + lax.ppermute(send0, "par", swap(par, 1))
    pair1 = keep1 + lax.ppermute(send1, "par", swap(par, 1))
    come = [over_pairs(pair0, d) for d in range(1, par // 2)]
    mine0 = pair0[:shard_rows] + sum(come[1:], come[0])
    mine1 = pair1[:shard_rows] + sum(over_pairs(pair1, d) for d in range(1, par // 2))
    gathered = over_sens(mine0) + over_sens(mine1)

    result = jax.ShapeDtypeStruct((cols, rows_dev), F32)
    partial = pl.pallas_call(
        functools.partial(update_kernel, packing, len(ready)),
        in_specs=[outside] * (2 * len(ready)) + [whole(part) for part in gathered],
        out_shape=result,
        scratch_shapes=[
            pltpu.VMEM(moved.shape, BF16),
            pltpu.VMEM(moved.shape, BF16),
            pltpu.SemaphoreType.DMA((2, blocks)),
        ],
        compiler_params=pltpu.CompilerParams(vmem_limit_bytes=limit),
        cost_estimate=pl.CostEstimate(
            flops=6 * rows_dev * times * cols * width, bytes_accessed=4 * rows_dev * times * width, transcendentals=0
        ),
        name="update",
    )(*(pair[0] for pair in ready), *(pair[1] for pair in ready), *gathered)
    spread = lax.all_to_all(partial.reshape(par, cols // par, rows_dev), "par", 0, 0)
    return jnp.sum(spread, axis=0)


def solution(mesh):
    return jax.shard_map(
        shards,
        mesh=mesh,
        in_specs=(
            P(None, "sens", None),
            P(None, "sens", "par"),
            P(None, "sens", "par"),
            P(),
            P(),
            P("sens", "par", None),
        ),
        out_specs=P("par", "sens"),
        check_vma=False,
    )
```
